512 devices in a mesh: ctx: 256 (over z_lo, y, x, core), head: 2 (over z_hi).
Axes of the slice: x: 4, y: 8, z: 8 (z_hi: 2, z_lo: 4; z = z_hi * 4 + z_lo), core: 2. Of those that a mesh axis runs over, the one named last changes fastest.
Arguments:
- queries: bfloat16 [131072, 8, 128], P('ctx', 'head'), may hold values from -6 to 6
- keys: bfloat16 [131072, 128], P('ctx'), may hold values from -6 to 6
- values: bfloat16 [131072, 128], P('ctx'), may hold values from -6 to 6
- outputs: bfloat16 [131072, 8, 128], P('ctx', 'head'), may hold values from -4 to 4
- grad_out: bfloat16 [131072, 8, 128], P('ctx', 'head'), may hold values from -6 to 6
- lse: float32 [8, 131072], P('head', 'ctx'), may hold values from 4 to 6
- span_order: int32 [512], replicated, may hold values from 0 to 511, each once
Outputs:
- grad_queries: bfloat16 [131072, 8, 128], P('ctx', 'head')
- grad_keys: bfloat16 [131072, 128], P(('ctx', 'head'))
- grad_values: bfloat16 [131072, 128], P(('ctx', 'head'))
The draws below stay inside these ranges and needn't reach their ends.
Inputs may be any that keep to these rules, and one draw needn't show every extreme that they name: `span_order`: each number once; slots 2 d and 2 d + 1 are the two spans of 256 rows of index d of ctx.
All inputs are finite; a program needn't handle non-finite values.
Results may differ from the reference program's by a relative error of at most 0.0059.
Values may be sent and summed in bfloat16 or wider, within the bound.
No kernel may reach another device: no remote copies, remote signals or barrier semaphores. Data moves between devices by JAX's collectives and lax.ppermute only.
A program may use at most 64 MiB of HBM per device.

```python
import jax
import jax.numpy as jnp
from jax import lax

GROUP = 8
HD = 128
TOK_DEV = 512
TOKENS = 131072
N_CTX = 256


def level_of(rng, extent, cuts, low, high):
    level, own = 1.0, jax.random.fold_in(rng, 6)
    for axis_at, parts in cuts:
        draws = jnp.exp(jax.random.uniform(jax.random.fold_in(own, axis_at), (parts,), jnp.float32, low / len(cuts), high / len(cuts)))
        level = level * jnp.repeat(draws, extent[axis_at] // parts).reshape([-1 if axis == axis_at else 1 for axis in range(len(extent))])
    return level


def centred(own_key, extent, scale, limit, split=(), kind=jnp.bfloat16):
    result = jax.random.normal(own_key, extent, jnp.float32) * scale
    if len(split) > 0:
        result = level_of(own_key, extent, split, -0.22, 0.18) * result
    return jnp.clip(result, min=-limit, max=limit).astype(kind)


def setup_inputs(seed: int = 0) -> dict:
    key_list = jax.random.split(jax.random.key(seed), 8)
    queries = centred(key_list[0], (TOKENS, GROUP, HD), 1.0, 6.0, ((0, 256), (1, 2)))
    keys = centred(key_list[1], (TOKENS, HD), 1.0, 6.0, ((0, 256),))
    values = centred(key_list[2], (TOKENS, HD), 1.0, 6.0, ((0, 256),))
    outputs = centred(key_list[3], (TOKENS, GROUP, HD), 0.5, 4.0, ((0, 256), (1, 2)))
    grad_out = centred(key_list[4], (TOKENS, GROUP, HD), 1.0, 6.0, ((0, 256), (1, 2)))
    lse = jnp.clip(4.0 + 2.0 * jax.random.uniform(key_list[5], (GROUP, TOKENS), jnp.float32) ** level_of(key_list[5], (GROUP, TOKENS), ((0, 2), (1, 256)), -0.2, 0.2), 4.0, 6.0)
    span_order = jax.random.permutation(key_list[6], 2 * N_CTX).astype(jnp.int32)
    return {"queries": queries, "keys": keys, "values": values, "outputs": outputs, "grad_out": grad_out, "lse": lse, "span_order": span_order}


def block_terms(query, grad_rows, lse_rows, delta_rows, query_pos, key, value, key_pos):
    scale = HD ** -0.5
    query_f = query.astype(jnp.float32)
    grad_f = grad_rows.astype(jnp.float32)
    key_f = key.astype(jnp.float32)
    value_f = value.astype(jnp.float32)
    scores = jnp.einsum('rgh,kh->grk', query_f, key_f) * scale
    allowed = key_pos[None, None, :] <= query_pos[None, :, None]
    probs = jnp.where(allowed, jnp.exp(scores - lse_rows[:, :, None]), jnp.float32(0.0))
    dprobs = jnp.einsum('rgh,kh->grk', grad_f, value_f)
    dscores = (probs * (dprobs - delta_rows[:, :, None])).astype(jnp.bfloat16).astype(jnp.float32)
    probs_low = probs.astype(jnp.bfloat16).astype(jnp.float32)
    grad_value = jnp.einsum('grk,rgh->kh', probs_low, grad_f)
    grad_key = jnp.einsum('grk,rgh->kh', dscores, query_f) * scale
    grad_query = jnp.einsum('grk,kh->rgh', dscores, key_f) * scale
    return grad_query, grad_key, grad_value


def reference(queries, keys, values, outputs, grad_out, lse, span_order):
    half_rows = TOK_DEV // 2
    row_ids = jnp.arange(TOKENS, dtype=jnp.int32)
    pos = span_order[row_ids // half_rows] * half_rows + row_ids % half_rows
    delta = jnp.einsum('tgh,tgh->gt', grad_out.astype(jnp.float32), outputs.astype(jnp.float32))
    query_blocks = queries.reshape(N_CTX, TOK_DEV, GROUP, HD)
    grad_blocks = grad_out.reshape(N_CTX, TOK_DEV, GROUP, HD)
    lse_blocks = lse.reshape(GROUP, N_CTX, TOK_DEV).transpose(1, 0, 2)
    delta_blocks = delta.reshape(GROUP, N_CTX, TOK_DEV).transpose(1, 0, 2)
    key_blocks = keys.reshape(N_CTX, TOK_DEV, HD)
    value_blocks = values.reshape(N_CTX, TOK_DEV, HD)
    pos_blocks = pos.reshape(N_CTX, TOK_DEV)
    grad_q = jnp.zeros((N_CTX, TOK_DEV, GROUP, HD), jnp.float32)
    grad_k = jnp.zeros((N_CTX, TOK_DEV, HD), jnp.float32)
    grad_v = jnp.zeros((N_CTX, TOK_DEV, HD), jnp.float32)
    for offset in range(-2, 3):
        def one_block(device):
            source = (device + offset) % N_CTX
            return block_terms(query_blocks[device], grad_blocks[device], lse_blocks[device], delta_blocks[device], pos_blocks[device], key_blocks[source], value_blocks[source], pos_blocks[source])
        part_q, part_k, part_v = lax.map(one_block, jnp.arange(N_CTX, dtype=jnp.int32))
        grad_q = grad_q + part_q
        grad_k = grad_k + jnp.roll(part_k, offset, axis=0)
        grad_v = grad_v + jnp.roll(part_v, offset, axis=0)
    return (grad_q.reshape(TOKENS, GROUP, HD).astype(jnp.bfloat16), grad_k.reshape(TOKENS, HD).astype(jnp.bfloat16), grad_v.reshape(TOKENS, HD).astype(jnp.bfloat16))
```

```python
import functools

import jax
import jax.numpy as jnp
from jax import lax
from jax.experimental import pallas as pl
from jax.experimental.pallas import tpu as pltpu
from jax.sharding import PartitionSpec as P

F32 = jnp.float32
BF16 = jnp.bfloat16
LOG2E = 1.4426950408889634
SUB = 512
VMEM = pl.BlockSpec(memory_space=pltpu.VMEM)
SMEM = pl.BlockSpec(memory_space=pltpu.SMEM)


def dot(a, b, ca, cb):
    return lax.dot_general(a, b, (((ca,), (cb,)), ((), ())), preferred_element_type=F32)


def lane_ones(rows, low, high):
    lane = lax.broadcasted_iota(jnp.int32, (rows, 128), 1)
    return jnp.where((lane >= low) & (lane < high), 1.0, 0.0).astype(BF16)


def prep_kernel(grad_ref, out_ref, lse_ref, extra_ref, wide):
    heads, tokens = lse_ref.shape
    depth = grad_ref.shape[1]
    lse = lse_ref[...] * float(depth**0.5)
    turned = jnp.concatenate([lse, jnp.zeros((128 - heads, tokens), F32)], axis=0).T
    for g in range(heads):
        wide[pl.ds(g, tokens, stride=heads), :] = jnp.broadcast_to(
            turned[:, g : g + 1], (tokens, 128)
        )
    delta = jnp.sum(
        grad_ref[...].astype(F32) * out_ref[...].astype(F32), axis=1, keepdims=True
    )
    lane = lax.broadcasted_iota(jnp.int32, wide.shape, 1)
    rest = jnp.where(lane < 3, wide[...], delta)
    high = rest.astype(BF16).astype(F32)
    rest = rest - high
    mid = rest.astype(BF16).astype(F32)
    low = rest - mid
    place = jnp.where(lane < 3, lane, lane - 3)
    term = jnp.where(place == 0, high, jnp.where(place == 1, mid, low))
    extra_ref[...] = jnp.where(lane < 6, -term, 0.0).astype(BF16)


def prep(grad_rows, out_rows, lse):
    rows, depth = grad_rows.shape
    return pl.pallas_call(
        prep_kernel,
        out_shape=jax.ShapeDtypeStruct((rows, 128), BF16),
        in_specs=[VMEM] * 3,
        out_specs=VMEM,
        scratch_shapes=[pltpu.VMEM((rows, 128), F32)],
        compiler_params=pltpu.CompilerParams(vmem_limit_bytes=16 * 2**20),
        cost_estimate=pl.CostEstimate(flops=rows * 1024, bytes_accessed=rows * 768, transcendentals=0),
        name="prep",
    )(grad_rows, out_rows, lse)


def tile(q_ref, do_ref, x_ref, key, value, q_base, rows, mask=None):
    span, depth = key.shape
    exponent = float(depth**-0.5 * LOG2E)
    key_x = jnp.concatenate([key, lane_ones(span, 0, 3)], axis=1)
    value_x = jnp.concatenate([value, lane_ones(span, 3, 6)], axis=1)

    def front(i):
        at = pl.ds(pl.multiple_of(q_base + i * SUB, SUB), SUB)
        q, do, x = q_ref[at, :], do_ref[at, :], x_ref[at, :]
        p = jnp.exp2(dot(jnp.concatenate([q, x], axis=1), key_x, 1, 1) * exponent)
        if mask is not None:
            p = jnp.where(mask(i * SUB, SUB, span), p, 0.0)
        dp = dot(jnp.concatenate([do, x], axis=1), value_x, 1, 1)
        return at, q, do, p.astype(BF16), (p * dp).astype(BF16)

    dk, dv = None, None
    pieces = rows // SUB
    later = front(0)
    terms = []
    for i in range(pieces):
        at, q, do, p, ds = later
        if i + 1 < pieces:
            later = front(i + 1)
        yield_dq = dot(ds, key, 1, 0)
        terms.append((at, yield_dq))
        part_v, part_k = dot(do, p, 0, 0), dot(q, ds, 0, 0)
        dv = part_v if dv is None else dv + part_v
        dk = part_k if dk is None else dk + part_k
    return terms, dk, dv


def far_kernel(distances, first, span_ref, q_ref, do_ref, x_ref, kv_ref, *refs):
    if first:
        dq_ref, g_ref = refs
        dq_ref[...] = jnp.zeros_like(dq_ref)
    else:
        _, dq_ref, g_ref = refs
    count = lax.axis_size("ctx")
    me = lax.axis_index("ctx")
    sign = 1 - 2 * (me % 2)
    depth = q_ref.shape[1]
    tokens = kv_ref.shape[0] // (2 * len(distances))
    span = tokens // 2
    half = q_ref.shape[0] // 2
    q0, q1 = span_ref[2 * me], span_ref[2 * me + 1]

    def step(t, carry):
        chunk, j = t // 2, t % 2
        distance = distances[0] if len(distances) == 1 else jnp.where(chunk == 0, *distances)
        source = (me + sign * distance + count) % count
        k_id = span_ref[2 * source + j]
        at = pl.multiple_of(chunk * 2 * tokens + j * span, span)
        key = lambda: kv_ref[pl.ds(at, span), :]
        value = lambda: kv_ref[pl.ds(at + tokens, span), :]
        k_rows = pl.ds(pl.multiple_of(chunk * 2 * depth, depth), depth)
        v_rows = pl.ds(pl.multiple_of(chunk * 2 * depth + depth, depth), depth)
        lanes = pl.ds(pl.multiple_of(j * span, span), span)
        a0, a1 = k_id < q0, k_id < q1

        def run(base, rows):
            terms, dk, dv = tile(q_ref, do_ref, x_ref, key(), value(), base, rows)
            for rows_at, term in terms:
                dq_ref[rows_at, :] += term
            g_ref[k_rows, lanes] = dk.astype(g_ref.dtype)
            g_ref[v_rows, lanes] = dv.astype(g_ref.dtype)

        @pl.when(a0 & a1)
        def _():
            run(0, 2 * half)

        @pl.when(a0 != a1)
        def _():
            run(jnp.where(a1, half, 0), half)

        @pl.when(~(a0 | a1))
        def _():
            g_ref[k_rows, lanes] = jnp.zeros((depth, span), g_ref.dtype)
            g_ref[v_rows, lanes] = jnp.zeros((depth, span), g_ref.dtype)

        return carry

    lax.fori_loop(0, 2 * len(distances), step, 0)


def far(distances, spans, q, do, x, kv, dq, dtype, name):
    rows, depth = q.shape
    chunks = len(distances)
    tokens = kv.shape[0] // (2 * chunks)
    args = [spans, q, do, x, kv] + ([] if dq is None else [dq])
    return pl.pallas_call(
        functools.partial(far_kernel, distances, dq is None),
        out_shape=[
            jax.ShapeDtypeStruct((rows, depth), F32),
            jax.ShapeDtypeStruct((chunks * 2 * depth, tokens), dtype),
        ],
        in_specs=[SMEM] + [VMEM] * (len(args) - 1),
        out_specs=[VMEM, VMEM],
        input_output_aliases={} if dq is None else {5: 0},
        compiler_params=pltpu.CompilerParams(vmem_limit_bytes=24 * 2**20),
        cost_estimate=pl.CostEstimate(
            flops=chunks * 10 * rows * tokens * depth,
            bytes_accessed=chunks * 2**20,
            transcendentals=chunks * rows * tokens,
        ),
        name=name,
    )(*args)


def own_kernel(span_ref, q_ref, do_ref, x_ref, kv_ref, dqin_ref, dq_ref, g_ref, acc):
    me = lax.axis_index("ctx")
    depth = q_ref.shape[1]
    tokens = kv_ref.shape[0] // 2
    span = tokens // 2
    half = q_ref.shape[0] // 2
    heads = half // span
    later_first = span_ref[2 * me] > span_ref[2 * me + 1]

    def causal(base, rows, span):
        token = (base + lax.broadcasted_iota(jnp.int32, (rows, span), 0)) // heads
        return lax.broadcasted_iota(jnp.int32, (rows, span), 1) <= token

    def load(j):
        at = pl.multiple_of(j * span, span)
        return kv_ref[pl.ds(at, span), :], kv_ref[pl.ds(at + tokens, span), :]

    def step(j, carry):
        key, value = load(j)
        terms, dk, dv = tile(q_ref, do_ref, x_ref, key, value, j * half, half, causal)
        for rows_at, term in terms:
            acc[rows_at, :] = dqin_ref[rows_at, :] + term
        lanes = pl.ds(pl.multiple_of(j * span, span), span)
        g_ref[0:depth, lanes] = dk
        g_ref[depth : 2 * depth, lanes] = dv
        return carry

    lax.fori_loop(0, 2, step, 0)
    j = jnp.where(later_first, 1, 0)
    key, value = load(j)
    terms, dk, dv = tile(q_ref, do_ref, x_ref, key, value, (1 - j) * half, half)
    for rows_at, term in terms:
        acc[rows_at, :] += term
    lanes = pl.ds(pl.multiple_of(j * span, span), span)
    g_ref[0:depth, lanes] += dk
    g_ref[depth : 2 * depth, lanes] += dv
    dq_ref[...] = (acc[...] * float(depth**-0.5)).astype(dq_ref.dtype)


def own(spans, q, do, x, kv, dq):
    rows, depth = q.shape
    tokens = kv.shape[0] // 2
    return pl.pallas_call(
        own_kernel,
        out_shape=[
            jax.ShapeDtypeStruct((rows, depth), BF16),
            jax.ShapeDtypeStruct((2 * depth, tokens), F32),
        ],
        in_specs=[SMEM] + [VMEM] * 5,
        out_specs=[VMEM, VMEM],
        scratch_shapes=[pltpu.VMEM((rows, depth), F32)],
        compiler_params=pltpu.CompilerParams(vmem_limit_bytes=24 * 2**20),
        cost_estimate=pl.CostEstimate(
            flops=10 * rows * tokens * depth,
            bytes_accessed=2**20,
            transcendentals=rows * tokens,
        ),
        name="own",
    )(spans, q, do, x, kv, dq)


def add_kernel(a_ref, b_ref, o_ref):
    rows = o_ref.shape[0]
    o_ref[...] = (a_ref[...] + b_ref[pl.ds(rows, rows), :].astype(F32)).astype(BF16)


def add(a, b):
    return pl.pallas_call(
        add_kernel,
        out_shape=jax.ShapeDtypeStruct(a.shape, BF16),
        in_specs=[VMEM, VMEM],
        out_specs=VMEM,
        compiler_params=pltpu.CompilerParams(vmem_limit_bytes=8 * 2**20),
        name="add",
    )(a, b)


def merge_kernel(own_ref, a_ref, b_ref, c_ref, keep_ref, send_ref):
    rows, tokens = own_ref.shape
    half = tokens // 2
    head = lax.axis_index("head")

    def part(index):
        lanes = pl.ds(pl.multiple_of(index * half, half), half)
        return (
            own_ref[:, lanes]
            + a_ref[:, lanes].astype(F32)
            + b_ref[:, lanes].astype(F32)
            + c_ref[0:rows, lanes].astype(F32)
        )

    send_ref[...] = part(1 - head).astype(BF16)
    keep_ref[...] = part(head)


def merge(g, a, b, c):
    rows, tokens = g.shape
    return pl.pallas_call(
        merge_kernel,
        out_shape=[
            jax.ShapeDtypeStruct((rows, tokens // 2), F32),
            jax.ShapeDtypeStruct((rows, tokens // 2), BF16),
        ],
        in_specs=[VMEM] * 4,
        out_specs=[VMEM, VMEM],
        compiler_params=pltpu.CompilerParams(vmem_limit_bytes=8 * 2**20),
        name="merge",
    )(g, a, b, c)


def last_kernel(keep_ref, got_ref, dk_ref, dv_ref):
    total = keep_ref[...] + got_ref[...].astype(F32)
    depth = total.shape[0] // 2
    dk_ref[...] = (total[:depth].T * float(depth**-0.5)).astype(BF16)
    dv_ref[...] = total[depth:].T.astype(BF16)


def last(keep, got):
    rows, tokens = keep.shape
    shape = jax.ShapeDtypeStruct((tokens, rows // 2), BF16)
    return pl.pallas_call(
        last_kernel,
        out_shape=[shape, shape],
        in_specs=[VMEM, VMEM],
        out_specs=[VMEM, VMEM],
        compiler_params=pltpu.CompilerParams(vmem_limit_bytes=8 * 2**20),
        name="last",
    )(keep, got)


def local(queries, keys, values, outputs, grad_out, lse, span_order):
    tokens, heads, depth = queries.shape
    count = lax.axis_size("ctx")
    q = queries.reshape(tokens * heads, depth)
    do = grad_out.reshape(tokens * heads, depth)
    out = outputs.reshape(tokens * heads, depth)
    even, odd = range(0, count, 2), range(1, count, 2)
    over_two = [(d, (d + 2) % count) for d in even] + [(d, (d - 2) % count) for d in odd]
    back_two = [(b, a) for a, b in over_two]
    over_one = [(d, (d - 1) % count) for d in even] + [(d, (d + 1) % count) for d in odd]
    mates = [(d, d ^ 1) for d in range(count)]

    kv = jnp.concatenate([keys, values], axis=0)
    kv_b = lax.ppermute(kv, "ctx", over_one)
    kv_a = lax.ppermute(kv, "ctx", over_two)
    x = prep(do, out, lse)
    kv_cd = lax.ppermute(jnp.concatenate([kv, kv_b], axis=0), "ctx", mates)

    dq, g_a = far((-2,), span_order, q, do, x, kv_a, None, BF16, "far_a")
    got_a = lax.ppermute(g_a, "ctx", back_two)
    dq, g_cd = far((1, 2), span_order, q, do, x, kv_cd, dq, BF16, "far_cd")
    got_cd = lax.ppermute(g_cd, "ctx", mates)
    dq, g_b = far((-1,), span_order, q, do, x, kv_b, dq, F32, "far_b")
    got_b = lax.ppermute(add(g_b, got_cd), "ctx", over_one)
    dq, g_own = own(span_order, q, do, x, kv, dq)
    keep, send = merge(g_own, got_a, got_b, got_cd)
    got = lax.ppermute(send, "head", [(0, 1), (1, 0)])
    grad_k, grad_v = last(keep, got)
    return dq.reshape(tokens, heads, depth), grad_k, grad_v


def solution(mesh):
    return jax.shard_map(
        local,
        mesh=mesh,
        in_specs=(
            P("ctx", "head", None),
            P("ctx", None),
            P("ctx", None),
            P("ctx", "head", None),
            P("ctx", "head", None),
            P("head", "ctx"),
            P(),
        ),
        out_specs=(P("ctx", "head", None), P(("ctx", "head"), None), P(("ctx", "head"), None)),
        check_vma=False,
    )
```

```python
import functools

import jax
import jax.numpy as jnp
from jax import lax
from jax.experimental import pallas as pl
from jax.experimental.pallas import tpu as pltpu
from jax.sharding import PartitionSpec as P

F32 = jnp.float32
BF16 = jnp.bfloat16
LOG2E = 1.4426950408889634
SUB = 512
VMEM = pl.BlockSpec(memory_space=pltpu.VMEM)
SMEM = pl.BlockSpec(memory_space=pltpu.SMEM)


def dot(a, b, ca, cb):
    return lax.dot_general(a, b, (((ca,), (cb,)), ((), ())), preferred_element_type=F32)


def lane_ones(rows, low, high):
    lane = lax.broadcasted_iota(jnp.int32, (rows, 128), 1)
    return jnp.where((lane >= low) & (lane < high), 1.0, 0.0).astype(BF16)


def prep_kernel(grad_ref, out_ref, lse_ref, extra_ref, wide):
    heads, tokens = lse_ref.shape
    depth = grad_ref.shape[1]
    lse = lse_ref[...] * float(depth**0.5)
    turned = jnp.concatenate([lse, jnp.zeros((128 - heads, tokens), F32)], axis=0).T
    for g in range(heads):
        wide[pl.ds(g, tokens, stride=heads), :] = jnp.broadcast_to(
            turned[:, g : g + 1], (tokens, 128)
        )
    delta = jnp.sum(
        grad_ref[...].astype(F32) * out_ref[...].astype(F32), axis=1, keepdims=True
    )
    lane = lax.broadcasted_iota(jnp.int32, wide.shape, 1)
    rest = jnp.where(lane < 3, wide[...], delta)
    high = rest.astype(BF16).astype(F32)
    rest = rest - high
    mid = rest.astype(BF16).astype(F32)
    low = rest - mid
    place = jnp.where(lane < 3, lane, lane - 3)
    term = jnp.where(place == 0, high, jnp.where(place == 1, mid, low))
    extra_ref[...] = jnp.where(lane < 6, -term, 0.0).astype(BF16)


def prep(grad_rows, out_rows, lse):
    rows, depth = grad_rows.shape
    return pl.pallas_call(
        prep_kernel,
        out_shape=jax.ShapeDtypeStruct((rows, 128), BF16),
        in_specs=[VMEM] * 3,
        out_specs=VMEM,
        scratch_shapes=[pltpu.VMEM((rows, 128), F32)],
        compiler_params=pltpu.CompilerParams(vmem_limit_bytes=16 * 2**20),
        cost_estimate=pl.CostEstimate(flops=rows * 1024, bytes_accessed=rows * 768, transcendentals=0),
        name="prep",
    )(grad_rows, out_rows, lse)


def tile(q_ref, do_ref, x_ref, key, value, q_base, rows, mask=None):
    span, depth = key.shape
    exponent = float(depth**-0.5 * LOG2E)
    key_x = jnp.concatenate([key, lane_ones(span, 0, 3)], axis=1)
    value_x = jnp.concatenate([value, lane_ones(span, 3, 6)], axis=1)

    def front(i):
        at = pl.ds(pl.multiple_of(q_base + i * SUB, SUB), SUB)
        q, do, x = q_ref[at, :], do_ref[at, :], x_ref[at, :]
        p = jnp.exp2(dot(jnp.concatenate([q, x], axis=1), key_x, 1, 1) * exponent)
        if mask is not None:
            p = jnp.where(mask(i * SUB, SUB, span), p, 0.0)
        dp = dot(jnp.concatenate([do, x], axis=1), value_x, 1, 1)
        return at, q, do, p.astype(BF16), (p * dp).astype(BF16)

    dk, dv = None, None
    pieces = rows // SUB
    later = front(0)
    terms = []
    for i in range(pieces):
        at, q, do, p, ds = later
        if i + 1 < pieces:
            later = front(i + 1)
        yield_dq = dot(ds, key, 1, 0)
        terms.append((at, yield_dq))
        part_v, part_k = dot(do, p, 0, 0), dot(q, ds, 0, 0)
        dv = part_v if dv is None else dv + part_v
        dk = part_k if dk is None else dk + part_k
    return terms, dk, dv


def far_kernel(distances, first, span_ref, q_ref, do_ref, x_ref, kv_ref, *refs):
    if first:
        dq_ref, g_ref = refs
        dq_ref[...] = jnp.zeros_like(dq_ref)
    else:
        _, dq_ref, g_ref = refs
    count = lax.axis_size("ctx")
    me = lax.axis_index("ctx")
    sign = 1 - 2 * (me % 2)
    depth = q_ref.shape[1]
    tokens = kv_ref.shape[0] // (2 * len(distances))
    span = tokens // 2
    half = q_ref.shape[0] // 2
    q0, q1 = span_ref[2 * me], span_ref[2 * me + 1]

    def step(t, carry):
        chunk, j = t // 2, t % 2
        distance = distances[0] if len(distances) == 1 else jnp.where(chunk == 0, *distances)
        source = (me + sign * distance + count) % count
        k_id = span_ref[2 * source + j]
        at = pl.multiple_of(chunk * 2 * tokens + j * span, span)
        key = lambda: kv_ref[pl.ds(at, span), :]
        value = lambda: kv_ref[pl.ds(at + tokens, span), :]
        k_rows = pl.ds(pl.multiple_of(chunk * 2 * depth, depth), depth)
        v_rows = pl.ds(pl.multiple_of(chunk * 2 * depth + depth, depth), depth)
        lanes = pl.ds(pl.multiple_of(j * span, span), span)
        a0, a1 = k_id < q0, k_id < q1

        def run(base, rows):
            terms, dk, dv = tile(q_ref, do_ref, x_ref, key(), value(), base, rows)
            for rows_at, term in terms:
                dq_ref[rows_at, :] += term
            g_ref[k_rows, lanes] = dk.astype(g_ref.dtype)
            g_ref[v_rows, lanes] = dv.astype(g_ref.dtype)

        @pl.when(a0 & a1)
        def _():
            run(0, 2 * half)

        @pl.when(a0 != a1)
        def _():
            run(jnp.where(a1, half, 0), half)

        @pl.when(~(a0 | a1))
        def _():
            g_ref[k_rows, lanes] = jnp.zeros((depth, span), g_ref.dtype)
            g_ref[v_rows, lanes] = jnp.zeros((depth, span), g_ref.dtype)

        return carry

    lax.fori_loop(0, 2 * len(distances), step, 0)


def far(distances, spans, q, do, x, kv, dq, dtype, name):
    rows, depth = q.shape
    chunks = len(distances)
    tokens = kv.shape[0] // (2 * chunks)
    args = [spans, q, do, x, kv] + ([] if dq is None else [dq])
    return pl.pallas_call(
        functools.partial(far_kernel, distances, dq is None),
        out_shape=[
            jax.ShapeDtypeStruct((rows, depth), F32),
            jax.ShapeDtypeStruct((chunks * 2 * depth, tokens), dtype),
        ],
        in_specs=[SMEM] + [VMEM] * (len(args) - 1),
        out_specs=[VMEM, VMEM],
        input_output_aliases={} if dq is None else {5: 0},
        compiler_params=pltpu.CompilerParams(vmem_limit_bytes=24 * 2**20),
        cost_estimate=pl.CostEstimate(
            flops=chunks * 10 * rows * tokens * depth,
            bytes_accessed=chunks * 2**20,
            transcendentals=chunks * rows * tokens,
        ),
        name=name,
    )(*args)


def own_kernel(span_ref, q_ref, do_ref, x_ref, kv_ref, dqin_ref, dq_ref, g_ref, acc):
    me = lax.axis_index("ctx")
    depth = q_ref.shape[1]
    tokens = kv_ref.shape[0] // 2
    span = tokens // 2
    half = q_ref.shape[0] // 2
    heads = half // span
    later_first = span_ref[2 * me] > span_ref[2 * me + 1]

    def causal(base, rows, span):
        token = (base + lax.broadcasted_iota(jnp.int32, (rows, span), 0)) // heads
        return lax.broadcasted_iota(jnp.int32, (rows, span), 1) <= token

    def load(j):
        at = pl.multiple_of(j * span, span)
        return kv_ref[pl.ds(at, span), :], kv_ref[pl.ds(at + tokens, span), :]

    def step(j, carry):
        key, value = load(j)
        terms, dk, dv = tile(q_ref, do_ref, x_ref, key, value, j * half, half, causal)
        for rows_at, term in terms:
            acc[rows_at, :] = dqin_ref[rows_at, :] + term
        lanes = pl.ds(pl.multiple_of(j * span, span), span)
        g_ref[0:depth, lanes] = dk
        g_ref[depth : 2 * depth, lanes] = dv
        return carry

    lax.fori_loop(0, 2, step, 0)
    j = jnp.where(later_first, 1, 0)
    key, value = load(j)
    terms, dk, dv = tile(q_ref, do_ref, x_ref, key, value, (1 - j) * half, half)
    for rows_at, term in terms:
        acc[rows_at, :] += term
    lanes = pl.ds(pl.multiple_of(j * span, span), span)
    g_ref[0:depth, lanes] += dk
    g_ref[depth : 2 * depth, lanes] += dv
    dq_ref[...] = (acc[...] * float(depth**-0.5)).astype(dq_ref.dtype)


def own(spans, q, do, x, kv, dq):
    rows, depth = q.shape
    tokens = kv.shape[0] // 2
    return pl.pallas_call(
        own_kernel,
        out_shape=[
            jax.ShapeDtypeStruct((rows, depth), BF16),
            jax.ShapeDtypeStruct((2 * depth, tokens), F32),
        ],
        in_specs=[SMEM] + [VMEM] * 5,
        out_specs=[VMEM, VMEM],
        scratch_shapes=[pltpu.VMEM((rows, depth), F32)],
        compiler_params=pltpu.CompilerParams(vmem_limit_bytes=24 * 2**20),
        cost_estimate=pl.CostEstimate(
            flops=10 * rows * tokens * depth,
            bytes_accessed=2**20,
            transcendentals=rows * tokens,
        ),
        name="own",
    )(spans, q, do, x, kv, dq)


def add_kernel(a_ref, b_ref, o_ref):
    rows = o_ref.shape[0]
    o_ref[...] = (a_ref[...] + b_ref[pl.ds(rows, rows), :].astype(F32)).astype(BF16)


def add(a, b):
    return pl.pallas_call(
        add_kernel,
        out_shape=jax.ShapeDtypeStruct(a.shape, BF16),
        in_specs=[VMEM, VMEM],
        out_specs=VMEM,
        compiler_params=pltpu.CompilerParams(vmem_limit_bytes=8 * 2**20),
        name="add",
    )(a, b)


def merge_kernel(own_ref, a_ref, b_ref, c_ref, keep_ref, send_ref):
    rows, tokens = own_ref.shape
    half = tokens // 2
    head = lax.axis_index("head")

    def part(index):
        lanes = pl.ds(pl.multiple_of(index * half, half), half)
        return (
            own_ref[:, lanes]
            + a_ref[:, lanes].astype(F32)
            + b_ref[:, lanes].astype(F32)
            + c_ref[0:rows, lanes].astype(F32)
        )

    send_ref[...] = part(1 - head).astype(BF16)
    keep_ref[...] = part(head)


def merge(g, a, b, c):
    rows, tokens = g.shape
    return pl.pallas_call(
        merge_kernel,
        out_shape=[
            jax.ShapeDtypeStruct((rows, tokens // 2), F32),
            jax.ShapeDtypeStruct((rows, tokens // 2), BF16),
        ],
        in_specs=[VMEM] * 4,
        out_specs=[VMEM, VMEM],
        compiler_params=pltpu.CompilerParams(vmem_limit_bytes=8 * 2**20),
        name="merge",
    )(g, a, b, c)


def last_kernel(keep_ref, got_ref, dk_ref, dv_ref):
    total = keep_ref[...] + got_ref[...].astype(F32)
    depth = total.shape[0] // 2
    dk_ref[...] = (total[:depth].T * float(depth**-0.5)).astype(BF16)
    dv_ref[...] = total[depth:].T.astype(BF16)


def last(keep, got):
    rows, tokens = keep.shape
    shape = jax.ShapeDtypeStruct((tokens, rows // 2), BF16)
    return pl.pallas_call(
        last_kernel,
        out_shape=[shape, shape],
        in_specs=[VMEM, VMEM],
        out_specs=[VMEM, VMEM],
        compiler_params=pltpu.CompilerParams(vmem_limit_bytes=8 * 2**20),
        name="last",
    )(keep, got)


def pack_kernel(a_ref, b_ref, _, o_ref):
    rows = a_ref.shape[0]
    o_ref[0:rows, :] = a_ref[...]
    o_ref[rows : 2 * rows, :] = b_ref[...]


def pack(a, b, after):
    rows, depth = a.shape
    return pl.pallas_call(
        pack_kernel,
        out_shape=jax.ShapeDtypeStruct((2 * rows, depth), a.dtype),
        in_specs=[VMEM, VMEM, pl.BlockSpec(memory_space=pl.ANY)],
        out_specs=VMEM,
        compiler_params=pltpu.CompilerParams(vmem_limit_bytes=8 * 2**20),
        name="pack",
    )(a, b, after)


def ring(count, move):
    pairs = []
    for d in range(count):
        target = move(d)
        flip = 0 if 0 <= target < count else 1
        for h in range(2):
            pairs.append((2 * d + h, 2 * (target % count) + (h ^ flip)))
    return pairs


def local(queries, keys, values, outputs, grad_out, lse, span_order):
    tokens, heads, depth = queries.shape
    count = lax.axis_size("ctx")
    both = ("ctx", "head")
    q = queries.reshape(tokens * heads, depth)
    do = grad_out.reshape(tokens * heads, depth)
    out = outputs.reshape(tokens * heads, depth)
    over_two = ring(count, lambda d: d - 2 if d % 2 else d + 2)
    back_two = [(b, a) for a, b in over_two]
    over_one = ring(count, lambda d: d + 1 if d % 2 else d - 1)
    mates = [(d, d ^ 1) for d in range(count)]

    kv = jnp.concatenate([keys, values], axis=0)
    kv_a = lax.ppermute(kv, both, over_two)
    kv_b = lax.ppermute(kv, both, over_one)
    x = prep(do, out, lse)

    dq, g_a = far((-2,), span_order, q, do, x, kv_a, None, BF16, "far_a")
    kv_cd = lax.ppermute(pack(kv, kv_b, g_a), "ctx", mates)
    got_a = lax.ppermute(g_a, both, back_two)
    dq, g_b = far((-1,), span_order, q, do, x, kv_b, dq, F32, "far_b")
    dq, g_cd = far((1, 2), span_order, q, do, x, kv_cd, dq, BF16, "far_cd")
    got_cd = lax.ppermute(g_cd, "ctx", mates)
    got_b = lax.ppermute(add(g_b, got_cd), both, over_one)
    dq, g_own = own(span_order, q, do, x, kv, dq)
    keep, send = merge(g_own, got_a, got_b, got_cd)
    got = lax.ppermute(send, "head", [(0, 1), (1, 0)])
    grad_k, grad_v = last(keep, got)
    return dq.reshape(tokens, heads, depth), grad_k, grad_v


def solution(mesh):
    return jax.shard_map(
        local,
        mesh=mesh,
        in_specs=(
            P("ctx", "head", None),
            P("ctx", None),
            P("ctx", None),
            P("ctx", "head", None),
            P("ctx", "head", None),
            P("head", "ctx"),
            P(),
        ),
        out_specs=(P("ctx", "head", None), P(("ctx", "head"), None), P(("ctx", "head"), None)),
        check_vma=False,
    )
```

```python
import functools

import jax
import jax.numpy as jnp
from jax import lax
from jax.experimental import pallas as pl
from jax.experimental.pallas import tpu as pltpu
from jax.sharding import PartitionSpec as P

F32 = jnp.float32
BF16 = jnp.bfloat16
LOG2E = 1.4426950408889634
SUB = 512
VMEM = pl.BlockSpec(memory_space=pltpu.VMEM)
SMEM = pl.BlockSpec(memory_space=pltpu.SMEM)


def dot(a, b, ca, cb):
    return lax.dot_general(a, b, (((ca,), (cb,)), ((), ())), preferred_element_type=F32)


def lane_ones(rows, low, high):
    lane = lax.broadcasted_iota(jnp.int32, (rows, 128), 1)
    return jnp.where((lane >= low) & (lane < high), 1.0, 0.0).astype(BF16)


def load_kernel(k_ref, v_ref, q_ref, do_ref, out_ref, kv_to, q_to, do_to, out_to, sems):
    rows = k_ref.shape[0]
    copies = [
        pltpu.make_async_copy(source, target, sems.at[i])
        for i, (source, target) in enumerate(
            [
                (k_ref, kv_to.at[pl.ds(0, rows)]),
                (v_ref, kv_to.at[pl.ds(rows, rows)]),
                (do_ref, do_to),
                (out_ref, out_to),
                (q_ref, q_to),
            ]
        )
    ]
    for copy in copies:
        copy.start()
    for copy in copies:
        copy.wait()


def load(keys, values, q, do, out):
    rows, depth = keys.shape
    wide = jax.ShapeDtypeStruct(q.shape, q.dtype)
    return pl.pallas_call(
        load_kernel,
        out_shape=[jax.ShapeDtypeStruct((2 * rows, depth), keys.dtype)] + [wide] * 3,
        in_specs=[pl.BlockSpec(memory_space=pltpu.HBM)] * 5,
        out_specs=[VMEM] * 4,
        scratch_shapes=[pltpu.SemaphoreType.DMA((5,))],
        compiler_params=pltpu.CompilerParams(vmem_limit_bytes=8 * 2**20),
        name="load",
    )(keys, values, q, do, out)


def prep_kernel(grad_ref, out_ref, lse_ref, extra_ref, wide):
    heads, tokens = lse_ref.shape
    depth = grad_ref.shape[1]
    lse = lse_ref[...] * float(depth**0.5)
    turned = jnp.concatenate([lse, jnp.zeros((128 - heads, tokens), F32)], axis=0).T
    for g in range(heads):
        wide[pl.ds(g, tokens, stride=heads), :] = jnp.broadcast_to(
            turned[:, g : g + 1], (tokens, 128)
        )
    delta = jnp.sum(
        grad_ref[...].astype(F32) * out_ref[...].astype(F32), axis=1, keepdims=True
    )
    lane = lax.broadcasted_iota(jnp.int32, wide.shape, 1)
    rest = jnp.where(lane < 3, wide[...], delta)
    high = rest.astype(BF16).astype(F32)
    rest = rest - high
    mid = rest.astype(BF16).astype(F32)
    low = rest - mid
    place = jnp.where(lane < 3, lane, lane - 3)
    term = jnp.where(place == 0, high, jnp.where(place == 1, mid, low))
    extra_ref[...] = jnp.where(lane < 6, -term, 0.0).astype(BF16)


def prep(grad_rows, out_rows, lse):
    rows, depth = grad_rows.shape
    return pl.pallas_call(
        prep_kernel,
        out_shape=jax.ShapeDtypeStruct((rows, 128), BF16),
        in_specs=[VMEM] * 3,
        out_specs=VMEM,
        scratch_shapes=[pltpu.VMEM((rows, 128), F32)],
        compiler_params=pltpu.CompilerParams(vmem_limit_bytes=16 * 2**20),
        cost_estimate=pl.CostEstimate(flops=rows * 1024, bytes_accessed=rows * 768, transcendentals=0),
        name="prep",
    )(grad_rows, out_rows, lse)


def tile(q_ref, do_ref, x_ref, key, value, q_base, rows, mask=None):
    span, depth = key.shape
    exponent = float(depth**-0.5 * LOG2E)
    key_x = jnp.concatenate([key, lane_ones(span, 0, 3)], axis=1)
    value_x = jnp.concatenate([value, lane_ones(span, 3, 6)], axis=1)

    def front(i):
        at = pl.ds(pl.multiple_of(q_base + i * SUB, SUB), SUB)
        q, do, x = q_ref[at, :], do_ref[at, :], x_ref[at, :]
        p = jnp.exp2(dot(jnp.concatenate([q, x], axis=1), key_x, 1, 1) * exponent)
        if mask is not None:
            p = jnp.where(mask(i * SUB, SUB, span), p, 0.0)
        dp = dot(jnp.concatenate([do, x], axis=1), value_x, 1, 1)
        return at, q, do, p.astype(BF16), (p * dp).astype(BF16)

    dk, dv = None, None
    pieces = rows // SUB
    later = front(0)
    terms = []
    for i in range(pieces):
        at, q, do, p, ds = later
        if i + 1 < pieces:
            later = front(i + 1)
        yield_dq = dot(ds, key, 1, 0)
        terms.append((at, yield_dq))
        part_v, part_k = dot(do, p, 0, 0), dot(q, ds, 0, 0)
        dv = part_v if dv is None else dv + part_v
        dk = part_k if dk is None else dk + part_k
    return terms, dk, dv


def far_kernel(distances, first, span_ref, q_ref, do_ref, x_ref, kv_ref, *refs):
    if first:
        dq_ref, g_ref = refs
        dq_ref[...] = jnp.zeros_like(dq_ref)
    else:
        _, dq_ref, g_ref = refs
    count = lax.axis_size("ctx")
    me = lax.axis_index("ctx")
    sign = 1 - 2 * (me % 2)
    depth = q_ref.shape[1]
    tokens = kv_ref.shape[0] // (2 * len(distances))
    span = tokens // 2
    half = q_ref.shape[0] // 2
    q0, q1 = span_ref[2 * me], span_ref[2 * me + 1]

    def run(base, rows, at, keys, k_rows, v_rows, lanes):
        key, value = kv_ref[pl.ds(at, keys), :], kv_ref[pl.ds(at + tokens, keys), :]
        terms, dk, dv = tile(q_ref, do_ref, x_ref, key, value, base, rows)
        for rows_at, term in terms:
            dq_ref[rows_at, :] += term
        g_ref[k_rows, lanes] = dk.astype(g_ref.dtype)
        g_ref[v_rows, lanes] = dv.astype(g_ref.dtype)

    def block(chunk, carry):
        distance = distances[0] if len(distances) == 1 else jnp.where(chunk == 0, *distances)
        source = (me + sign * distance + count) % count
        k0, k1 = span_ref[2 * source], span_ref[2 * source + 1]
        first_row = pl.multiple_of(chunk * 2 * tokens, 2 * tokens)
        k_rows = pl.ds(pl.multiple_of(chunk * 2 * depth, depth), depth)
        v_rows = pl.ds(pl.multiple_of(chunk * 2 * depth + depth, depth), depth)
        every = jnp.maximum(k0, k1) < jnp.minimum(q0, q1)

        @pl.when(every)
        def _():
            run(0, 2 * half, first_row, tokens, k_rows, v_rows, pl.ds(0, tokens))

        def one_span(j, carry):
            k_id = jnp.where(j == 0, k0, k1)
            at = pl.multiple_of(first_row + j * span, span)
            lanes = pl.ds(pl.multiple_of(j * span, span), span)
            a0, a1 = k_id < q0, k_id < q1

            @pl.when(a0 & a1)
            def _():
                run(0, 2 * half, at, span, k_rows, v_rows, lanes)

            @pl.when(a0 != a1)
            def _():
                run(jnp.where(a1, half, 0), half, at, span, k_rows, v_rows, lanes)

            @pl.when(~(a0 | a1))
            def _():
                g_ref[k_rows, lanes] = jnp.zeros((depth, span), g_ref.dtype)
                g_ref[v_rows, lanes] = jnp.zeros((depth, span), g_ref.dtype)

            return carry

        @pl.when(~every)
        def _():
            lax.fori_loop(0, 2, one_span, 0)

        return carry

    if len(distances) == 1:
        block(0, 0)
    else:
        lax.fori_loop(0, len(distances), block, 0)


def far(distances, spans, q, do, x, kv, dq, dtype, name):
    rows, depth = q.shape
    chunks = len(distances)
    tokens = kv.shape[0] // (2 * chunks)
    args = [spans, q, do, x, kv] + ([] if dq is None else [dq])
    return pl.pallas_call(
        functools.partial(far_kernel, distances, dq is None),
        out_shape=[
            jax.ShapeDtypeStruct((rows, depth), F32),
            jax.ShapeDtypeStruct((chunks * 2 * depth, tokens), dtype),
        ],
        in_specs=[SMEM] + [VMEM] * (len(args) - 1),
        out_specs=[VMEM, VMEM],
        input_output_aliases={} if dq is None else {5: 0},
        compiler_params=pltpu.CompilerParams(vmem_limit_bytes=24 * 2**20),
        cost_estimate=pl.CostEstimate(
            flops=chunks * 10 * rows * tokens * depth,
            bytes_accessed=chunks * 2**20,
            transcendentals=chunks * rows * tokens,
        ),
        name=name,
    )(*args)


def own_low_kernel(span_ref, q_ref, do_ref, x_ref, kv_ref, _, dq_ref, g_ref):
    me = lax.axis_index("ctx")
    depth = q_ref.shape[1]
    tokens = kv_ref.shape[0] // 2
    span, half = tokens // 2, q_ref.shape[0] // 2
    heads = half // span
    low = jnp.where(span_ref[2 * me] > span_ref[2 * me + 1], 1, 0)

    def causal(base, rows, keys):
        token = (base + lax.broadcasted_iota(jnp.int32, (rows, keys), 0)) // heads
        return lax.broadcasted_iota(jnp.int32, (rows, keys), 1) <= token

    at = pl.multiple_of(low * span, span)
    key, value = kv_ref[pl.ds(at, span), :], kv_ref[pl.ds(at + tokens, span), :]
    terms, dk, dv = tile(q_ref, do_ref, x_ref, key, value, low * half, half, causal)
    for rows_at, term in terms:
        dq_ref[rows_at, :] += term
    g_ref[0:depth, :] = dk
    g_ref[depth : 2 * depth, :] = dv


def own_high_kernel(span_ref, q_ref, do_ref, x_ref, kv_ref, g_low_ref, _, dq_ref, g_ref):
    me = lax.axis_index("ctx")
    depth = q_ref.shape[1]
    tokens = kv_ref.shape[0] // 2
    span, half = tokens // 2, q_ref.shape[0] // 2
    heads = half // span
    low = jnp.where(span_ref[2 * me] > span_ref[2 * me + 1], 1, 0)

    def causal(base, rows, keys):
        token = (base + lax.broadcasted_iota(jnp.int32, (rows, keys), 0)) // heads
        slot = lax.broadcasted_iota(jnp.int32, (rows, keys), 1)
        return (slot - (1 - low) * span <= token) & ((slot >= span) | (low == 1)) | (
            (slot // span) == low
        )

    terms, dk, dv = tile(
        q_ref, do_ref, x_ref, kv_ref[0:tokens, :], kv_ref[tokens : 2 * tokens, :],
        (1 - low) * half, half, causal,
    )
    for rows_at, term in terms:
        dq_ref[rows_at, :] += term
    g_ref[0:depth, :] = dk
    g_ref[depth : 2 * depth, :] = dv
    lanes = pl.ds(pl.multiple_of(low * span, span), span)
    g_ref[:, lanes] += g_low_ref[...]


def own(kernel, spans, q, do, x, kv, extra, dq, keys, name):
    rows, depth = q.shape
    args = [spans, q, do, x, kv] + extra + [dq]
    return pl.pallas_call(
        kernel,
        out_shape=[
            jax.ShapeDtypeStruct((rows, depth), F32),
            jax.ShapeDtypeStruct((2 * depth, keys), F32),
        ],
        in_specs=[SMEM] + [VMEM] * (len(args) - 1),
        out_specs=[VMEM, VMEM],
        input_output_aliases={len(args) - 1: 0},
        compiler_params=pltpu.CompilerParams(vmem_limit_bytes=24 * 2**20),
        cost_estimate=pl.CostEstimate(
            flops=5 * rows * keys * depth, bytes_accessed=2**20, transcendentals=rows * keys // 2
        ),
        name=name,
    )(*args)


def finish_kernel(dq_ref, o_ref):
    o_ref[...] = (dq_ref[...] * float(dq_ref.shape[1] ** -0.5)).astype(BF16)


def finish(dq):
    return pl.pallas_call(
        finish_kernel,
        out_shape=jax.ShapeDtypeStruct(dq.shape, BF16),
        in_specs=[VMEM],
        out_specs=VMEM,
        compiler_params=pltpu.CompilerParams(vmem_limit_bytes=8 * 2**20),
        cost_estimate=pl.CostEstimate(flops=dq.size, bytes_accessed=6 * dq.size, transcendentals=0),
        name="finish",
    )(dq)


def add_kernel(a_ref, b_ref, o_ref):
    rows = o_ref.shape[0]
    o_ref[...] = (a_ref[...] + b_ref[pl.ds(rows, rows), :].astype(F32)).astype(BF16)


def add(a, b):
    return pl.pallas_call(
        add_kernel,
        out_shape=jax.ShapeDtypeStruct(a.shape, BF16),
        in_specs=[VMEM, VMEM],
        out_specs=VMEM,
        compiler_params=pltpu.CompilerParams(vmem_limit_bytes=8 * 2**20),
        name="add",
    )(a, b)


def merge_kernel(own_ref, a_ref, b_ref, c_ref, keep_ref, send_ref):
    rows, tokens = own_ref.shape
    half = tokens // 2
    head = lax.axis_index("head")

    def part(index):
        lanes = pl.ds(pl.multiple_of(index * half, half), half)
        return (
            own_ref[:, lanes]
            + a_ref[:, lanes].astype(F32)
            + b_ref[:, lanes].astype(F32)
            + c_ref[0:rows, lanes].astype(F32)
        )

    send_ref[...] = part(1 - head).astype(BF16)
    keep_ref[...] = part(head)


def merge(g, a, b, c):
    rows, tokens = g.shape
    return pl.pallas_call(
        merge_kernel,
        out_shape=[
            jax.ShapeDtypeStruct((rows, tokens // 2), F32),
            jax.ShapeDtypeStruct((rows, tokens // 2), BF16),
        ],
        in_specs=[VMEM] * 4,
        out_specs=[VMEM, VMEM],
        compiler_params=pltpu.CompilerParams(vmem_limit_bytes=8 * 2**20),
        name="merge",
    )(g, a, b, c)


def last_kernel(keep_ref, got_ref, dk_ref, dv_ref):
    total = keep_ref[...] + got_ref[...].astype(F32)
    depth = total.shape[0] // 2
    dk_ref[...] = (total[:depth].T * float(depth**-0.5)).astype(BF16)
    dv_ref[...] = total[depth:].T.astype(BF16)


def last(keep, got):
    rows, tokens = keep.shape
    shape = jax.ShapeDtypeStruct((tokens, rows // 2), BF16)
    return pl.pallas_call(
        last_kernel,
        out_shape=[shape, shape],
        in_specs=[VMEM, VMEM],
        out_specs=[VMEM, VMEM],
        compiler_params=pltpu.CompilerParams(vmem_limit_bytes=8 * 2**20),
        name="last",
    )(keep, got)


def pack_kernel(a_ref, b_ref, _, o_ref):
    rows = a_ref.shape[0]
    o_ref[0:rows, :] = a_ref[...]
    o_ref[rows : 2 * rows, :] = b_ref[...]


def pack(a, b, after):
    rows, depth = a.shape
    return pl.pallas_call(
        pack_kernel,
        out_shape=jax.ShapeDtypeStruct((2 * rows, depth), a.dtype),
        in_specs=[VMEM, VMEM, pl.BlockSpec(memory_space=pl.ANY)],
        out_specs=VMEM,
        compiler_params=pltpu.CompilerParams(vmem_limit_bytes=8 * 2**20),
        name="pack",
    )(a, b, after)


def ring(count, move):
    pairs = []
    for d in range(count):
        target = move(d)
        flip = 0 if 0 <= target < count else 1
        for h in range(2):
            pairs.append((2 * d + h, 2 * (target % count) + (h ^ flip)))
    return pairs


def local(queries, keys, values, outputs, grad_out, lse, span_order):
    tokens, heads, depth = queries.shape
    count = lax.axis_size("ctx")
    both = ("ctx", "head")
    q = queries.reshape(tokens * heads, depth)
    do = grad_out.reshape(tokens * heads, depth)
    out = outputs.reshape(tokens * heads, depth)
    over_two = ring(count, lambda d: d - 2 if d % 2 else d + 2)
    back_two = [(b, a) for a, b in over_two]
    over_one = ring(count, lambda d: d + 1 if d % 2 else d - 1)
    mates = [(d, d ^ 1) for d in range(count)]

    kv, q, do, out = load(keys, values, q, do, out)
    kv_a = lax.ppermute(kv, both, over_two)
    kv_b = lax.ppermute(kv, both, over_one)
    x = prep(do, out, lse)

    dq, g_a = far((-2,), span_order, q, do, x, kv_a, None, BF16, "far_a")
    kv_cd = lax.ppermute(pack(kv, kv_b, g_a), "ctx", mates)
    got_a = lax.ppermute(g_a, both, back_two)
    dq, g_b = far((-1,), span_order, q, do, x, kv_b, dq, F32, "far_b")
    dq, g_cd = far((1, 2), span_order, q, do, x, kv_cd, dq, BF16, "far_cd")
    got_cd = lax.ppermute(g_cd, "ctx", mates)
    span = tokens // 2
    dq, g_low = own(own_low_kernel, span_order, q, do, x, kv, [], dq, span, "own_low")
    got_b = lax.ppermute(add(g_b, got_cd), both, over_one)
    dq, g_own = own(own_high_kernel, span_order, q, do, x, kv, [g_low], dq, tokens, "own_high")
    keep, send = merge(g_own, got_a, got_b, got_cd)
    got = lax.ppermute(send, "head", [(0, 1), (1, 0)])
    grad_q = finish(dq)
    grad_k, grad_v = last(keep, got)
    return grad_q.reshape(tokens, heads, depth), grad_k, grad_v


def solution(mesh):
    return jax.shard_map(
        local,
        mesh=mesh,
        in_specs=(
            P("ctx", "head", None),
            P("ctx", None),
            P("ctx", None),
            P("ctx", "head", None),
            P("ctx", "head", None),
            P("head", "ctx"),
            P(),
        ),
        out_specs=(P("ctx", "head", None), P(("ctx", "head"), None), P(("ctx", "head"), None)),
        check_vma=False,
    )
```

```python
import functools

import jax
import jax.numpy as jnp
from jax import lax
from jax.experimental import pallas as pl
from jax.experimental.pallas import tpu as pltpu
from jax.sharding import PartitionSpec as P

F32 = jnp.float32
BF16 = jnp.bfloat16
LOG2E = 1.4426950408889634
SUB = 512
VMEM = pl.BlockSpec(memory_space=pltpu.VMEM)
SMEM = pl.BlockSpec(memory_space=pltpu.SMEM)


def dot(a, b, ca, cb):
    return lax.dot_general(a, b, (((ca,), (cb,)), ((), ())), preferred_element_type=F32)


def lane_ones(rows, low, high):
    lane = lax.broadcasted_iota(jnp.int32, (rows, 128), 1)
    return jnp.where((lane >= low) & (lane < high), 1.0, 0.0).astype(BF16)


def load_kernel(k_ref, v_ref, q_ref, do_ref, out_ref, kv_to, q_to, do_to, out_to, sems):
    rows = k_ref.shape[0]
    copies = [
        pltpu.make_async_copy(source, target, sems.at[i])
        for i, (source, target) in enumerate(
            [
                (k_ref, kv_to.at[pl.ds(0, rows)]),
                (v_ref, kv_to.at[pl.ds(rows, rows)]),
                (do_ref, do_to),
                (out_ref, out_to),
                (q_ref, q_to),
            ]
        )
    ]
    for copy in copies:
        copy.start()
    for copy in copies:
        copy.wait()


def load(keys, values, q, do, out):
    rows, depth = keys.shape
    wide = jax.ShapeDtypeStruct(q.shape, q.dtype)
    args = [pltpu.with_memory_space_constraint(a, pltpu.HBM) for a in (keys, values, q, do, out)]
    return pl.pallas_call(
        load_kernel,
        out_shape=[jax.ShapeDtypeStruct((2 * rows, depth), keys.dtype)] + [wide] * 3,
        in_specs=[pl.BlockSpec(memory_space=pltpu.HBM)] * 5,
        out_specs=[VMEM] * 4,
        scratch_shapes=[pltpu.SemaphoreType.DMA((5,))],
        compiler_params=pltpu.CompilerParams(vmem_limit_bytes=8 * 2**20),
        name="load",
    )(*args)


def prep_kernel(grad_ref, out_ref, lse_ref, extra_ref, wide):
    heads, tokens = lse_ref.shape
    depth = grad_ref.shape[1]
    lse = lse_ref[...] * float(depth**0.5)
    turned = jnp.concatenate([lse, jnp.zeros((128 - heads, tokens), F32)], axis=0).T
    for g in range(heads):
        wide[pl.ds(g, tokens, stride=heads), :] = jnp.broadcast_to(
            turned[:, g : g + 1], (tokens, 128)
        )
    delta = jnp.sum(
        grad_ref[...].astype(F32) * out_ref[...].astype(F32), axis=1, keepdims=True
    )
    lane = lax.broadcasted_iota(jnp.int32, wide.shape, 1)
    rest = jnp.where(lane < 3, wide[...], delta)
    high = rest.astype(BF16).astype(F32)
    rest = rest - high
    mid = rest.astype(BF16).astype(F32)
    low = rest - mid
    place = jnp.where(lane < 3, lane, lane - 3)
    term = jnp.where(place == 0, high, jnp.where(place == 1, mid, low))
    extra_ref[...] = jnp.where(lane < 6, -term, 0.0).astype(BF16)


def prep(grad_rows, out_rows, lse):
    rows, depth = grad_rows.shape
    return pl.pallas_call(
        prep_kernel,
        out_shape=jax.ShapeDtypeStruct((rows, 128), BF16),
        in_specs=[VMEM] * 3,
        out_specs=VMEM,
        scratch_shapes=[pltpu.VMEM((rows, 128), F32)],
        compiler_params=pltpu.CompilerParams(vmem_limit_bytes=16 * 2**20),
        cost_estimate=pl.CostEstimate(flops=rows * 1024, bytes_accessed=rows * 768, transcendentals=0),
        name="prep",
    )(grad_rows, out_rows, lse)


def tile(q_ref, do_ref, x_ref, key, value, q_base, rows, mask=None):
    span, depth = key.shape
    exponent = float(depth**-0.5 * LOG2E)
    key_x = jnp.concatenate([key, lane_ones(span, 0, 3)], axis=1)
    value_x = jnp.concatenate([value, lane_ones(span, 3, 6)], axis=1)

    def front(i):
        at = pl.ds(pl.multiple_of(q_base + i * SUB, SUB), SUB)
        q, do, x = q_ref[at, :], do_ref[at, :], x_ref[at, :]
        p = jnp.exp2(dot(jnp.concatenate([q, x], axis=1), key_x, 1, 1) * exponent)
        if mask is not None:
            p = jnp.where(mask(i * SUB, SUB, span), p, 0.0)
        dp = dot(jnp.concatenate([do, x], axis=1), value_x, 1, 1)
        return at, q, do, p.astype(BF16), (p * dp).astype(BF16)

    dk, dv = None, None
    pieces = rows // SUB
    later = front(0)
    terms = []
    for i in range(pieces):
        at, q, do, p, ds = later
        if i + 1 < pieces:
            later = front(i + 1)
        yield_dq = dot(ds, key, 1, 0)
        terms.append((at, yield_dq))
        part_v, part_k = dot(do, p, 0, 0), dot(q, ds, 0, 0)
        dv = part_v if dv is None else dv + part_v
        dk = part_k if dk is None else dk + part_k
    return terms, dk, dv


def far_kernel(distance, index, first, span_ref, q_ref, do_ref, x_ref, kv_ref, *refs):
    dq_ref, g_ref = refs if first else refs[-2:]
    count = lax.axis_size("ctx")
    me = lax.axis_index("ctx")
    depth = q_ref.shape[1]
    tokens = g_ref.shape[1]
    span = tokens // 2
    half = q_ref.shape[0] // 2
    first_row = 2 * tokens * index
    source = (me + (1 - 2 * (me % 2)) * distance + count) % count
    q0, q1 = span_ref[2 * me], span_ref[2 * me + 1]
    k0, k1 = span_ref[2 * source], span_ref[2 * source + 1]
    every = jnp.maximum(k0, k1) < jnp.minimum(q0, q1)

    def run(base, rows, at, keys, lanes, store=False):
        key, value = kv_ref[pl.ds(at, keys), :], kv_ref[pl.ds(at + tokens, keys), :]
        terms, dk, dv = tile(q_ref, do_ref, x_ref, key, value, base, rows)
        for rows_at, term in terms:
            dq_ref[rows_at, :] = term if store else dq_ref[rows_at, :] + term
        g_ref[0:depth, lanes] = dk.astype(g_ref.dtype)
        g_ref[depth : 2 * depth, lanes] = dv.astype(g_ref.dtype)

    @pl.when(every)
    def _():
        run(0, 2 * half, first_row, tokens, pl.ds(0, tokens), store=first)

    def one_span(j, carry):
        k_id = jnp.where(j == 0, k0, k1)
        at = pl.multiple_of(first_row + j * span, span)
        lanes = pl.ds(pl.multiple_of(j * span, span), span)
        a0, a1 = k_id < q0, k_id < q1

        @pl.when(a0 & a1)
        def _():
            run(0, 2 * half, at, span, lanes)

        @pl.when(a0 != a1)
        def _():
            run(jnp.where(a1, half, 0), half, at, span, lanes)

        @pl.when(~(a0 | a1))
        def _():
            g_ref[:, lanes] = jnp.zeros((2 * depth, span), g_ref.dtype)

        return carry

    @pl.when(~every)
    def _():
        if first:
            dq_ref[...] = jnp.zeros_like(dq_ref)
        lax.fori_loop(0, 2, one_span, 0)


def far(distance, index, tokens, spans, q, do, x, kv, dq, dtype, name, after=None, weight=10):
    rows, depth = q.shape
    args = [spans, q, do, x, kv] + ([] if dq is None else [dq])
    order = [] if after is None else [after]
    return pl.pallas_call(
        functools.partial(far_kernel, distance, index, dq is None),
        out_shape=[
            jax.ShapeDtypeStruct((rows, depth), F32),
            jax.ShapeDtypeStruct((2 * depth, tokens), dtype),
        ],
        in_specs=[SMEM] + [VMEM] * (len(args) - 1) + [pl.BlockSpec(memory_space=pl.ANY)] * len(order),
        out_specs=[VMEM, VMEM],
        input_output_aliases={} if dq is None else {5: 0},
        compiler_params=pltpu.CompilerParams(vmem_limit_bytes=24 * 2**20),
        cost_estimate=pl.CostEstimate(
            flops=weight * rows * tokens * depth,
            bytes_accessed=2**16,
            transcendentals=weight * rows * tokens // 10,
        ),
        name=name,
    )(*args, *order)


def own_low_kernel(span_ref, q_ref, do_ref, x_ref, kv_ref, _, dq_ref, g_ref):
    me = lax.axis_index("ctx")
    depth = q_ref.shape[1]
    tokens = kv_ref.shape[0] // 2
    span, half = tokens // 2, q_ref.shape[0] // 2
    heads = half // span
    low = jnp.where(span_ref[2 * me] > span_ref[2 * me + 1], 1, 0)

    def causal(base, rows, keys):
        row = lax.broadcasted_iota(jnp.int32, (rows, keys), 0)
        return heads * lax.broadcasted_iota(jnp.int32, (rows, keys), 1) - row <= base

    at = pl.multiple_of(low * span, span)
    key, value = kv_ref[pl.ds(at, span), :], kv_ref[pl.ds(at + tokens, span), :]
    terms, dk, dv = tile(q_ref, do_ref, x_ref, key, value, low * half, half, causal)
    for rows_at, term in terms:
        dq_ref[rows_at, :] += term
    g_ref[0:depth, :] = dk
    g_ref[depth : 2 * depth, :] = dv


def own_high_kernel(span_ref, q_ref, do_ref, x_ref, kv_ref, g_low_ref, _, dq_ref, g_ref):
    me = lax.axis_index("ctx")
    depth = q_ref.shape[1]
    tokens = kv_ref.shape[0] // 2
    span, half = tokens // 2, q_ref.shape[0] // 2
    heads = half // span
    low = jnp.where(span_ref[2 * me] > span_ref[2 * me + 1], 1, 0)

    def causal(base, rows, keys):
        row = lax.broadcasted_iota(jnp.int32, (rows, keys), 0)
        slot = lax.broadcasted_iota(jnp.int32, (1, keys), 1)
        own = (slot >= span) == (low == 0)
        return jnp.where(own, heads * (slot & (span - 1)), -1) - row <= base

    terms, dk, dv = tile(
        q_ref, do_ref, x_ref, kv_ref[0:tokens, :], kv_ref[tokens : 2 * tokens, :],
        (1 - low) * half, half, causal,
    )
    for rows_at, term in terms:
        dq_ref[rows_at, :] += term
    g_ref[0:depth, :] = dk
    g_ref[depth : 2 * depth, :] = dv
    lanes = pl.ds(pl.multiple_of(low * span, span), span)
    g_ref[:, lanes] += g_low_ref[...]


def own(kernel, spans, q, do, x, kv, extra, dq, keys, name, weight):
    rows, depth = q.shape
    args = [spans, q, do, x, kv] + extra + [dq]
    return pl.pallas_call(
        kernel,
        out_shape=[
            jax.ShapeDtypeStruct((rows, depth), F32),
            jax.ShapeDtypeStruct((2 * depth, keys), F32),
        ],
        in_specs=[SMEM] + [VMEM] * (len(args) - 1),
        out_specs=[VMEM, VMEM],
        input_output_aliases={len(args) - 1: 0},
        compiler_params=pltpu.CompilerParams(vmem_limit_bytes=24 * 2**20),
        cost_estimate=pl.CostEstimate(
            flops=weight * rows * keys * depth, bytes_accessed=2**16, transcendentals=weight * rows * keys // 10
        ),
        name=name,
    )(*args)


def finish_kernel(dq_ref, o_ref):
    o_ref[...] = (dq_ref[...] * float(dq_ref.shape[1] ** -0.5)).astype(BF16)


def finish(dq):
    return pl.pallas_call(
        finish_kernel,
        out_shape=jax.ShapeDtypeStruct(dq.shape, BF16),
        in_specs=[VMEM],
        out_specs=VMEM,
        compiler_params=pltpu.CompilerParams(vmem_limit_bytes=8 * 2**20),
        cost_estimate=pl.CostEstimate(flops=dq.size, bytes_accessed=6 * dq.size, transcendentals=0),
        name="finish",
    )(dq)


def add_kernel(a_ref, b_ref, _, __, o_ref):
    rows = a_ref.shape[0]
    o_ref[0:rows, :] = (a_ref[...] + b_ref[...].astype(F32)).astype(BF16)
    o_ref[rows:, :] = jnp.zeros((o_ref.shape[0] - rows, o_ref.shape[1]), BF16)


def add(a, b, after, after_too):
    rows, tokens = a.shape
    return pl.pallas_call(
        add_kernel,
        out_shape=jax.ShapeDtypeStruct((rows + 16, tokens), BF16),
        in_specs=[VMEM, VMEM] + [pl.BlockSpec(memory_space=pl.ANY)] * 2,
        out_specs=VMEM,
        compiler_params=pltpu.CompilerParams(vmem_limit_bytes=8 * 2**20),
        name="add",
    )(a, b, after, after_too)


def merge_kernel(own_ref, a_ref, b_ref, c_ref, keep_ref, send_ref):
    rows, tokens = own_ref.shape
    half = tokens // 2
    head = lax.axis_index("head")

    def part(index):
        lanes = pl.ds(pl.multiple_of(index * half, half), half)
        return (
            own_ref[:, lanes]
            + a_ref[:, lanes].astype(F32)
            + b_ref[0:rows, lanes].astype(F32)
            + c_ref[:, lanes].astype(F32)
        )

    send_ref[...] = part(1 - head).astype(BF16)
    keep_ref[...] = part(head)


def merge(g, a, b, c):
    rows, tokens = g.shape
    return pl.pallas_call(
        merge_kernel,
        out_shape=[
            jax.ShapeDtypeStruct((rows, tokens // 2), F32),
            jax.ShapeDtypeStruct((rows, tokens // 2), BF16),
        ],
        in_specs=[VMEM] * 4,
        out_specs=[VMEM, VMEM],
        compiler_params=pltpu.CompilerParams(vmem_limit_bytes=8 * 2**20),
        name="merge",
    )(g, a, b, c)


def last_kernel(keep_ref, got_ref, dk_ref, dv_ref):
    total = keep_ref[...] + got_ref[...].astype(F32)
    depth = total.shape[0] // 2
    dk_ref[...] = (total[:depth].T * float(depth**-0.5)).astype(BF16)
    dv_ref[...] = total[depth:].T.astype(BF16)


def last(keep, got):
    rows, tokens = keep.shape
    shape = jax.ShapeDtypeStruct((tokens, rows // 2), BF16)
    return pl.pallas_call(
        last_kernel,
        out_shape=[shape, shape],
        in_specs=[VMEM, VMEM],
        out_specs=[VMEM, VMEM],
        compiler_params=pltpu.CompilerParams(vmem_limit_bytes=8 * 2**20),
        name="last",
    )(keep, got)


def pack_kernel(a_ref, b_ref, _, o_ref):
    rows = a_ref.shape[0]
    o_ref[0:rows, :] = a_ref[...]
    o_ref[rows : 2 * rows, :] = b_ref[...]


def pack(a, b, after):
    rows, depth = a.shape
    return pl.pallas_call(
        pack_kernel,
        out_shape=jax.ShapeDtypeStruct((2 * rows, depth), a.dtype),
        in_specs=[VMEM, VMEM, pl.BlockSpec(memory_space=pl.ANY)],
        out_specs=VMEM,
        compiler_params=pltpu.CompilerParams(vmem_limit_bytes=8 * 2**20),
        name="pack",
    )(a, b, after)


def ring(count, move):
    pairs = []
    for d in range(count):
        target = move(d)
        flip = 0 if 0 <= target < count else 1
        for h in range(2):
            pairs.append((2 * d + h, 2 * (target % count) + (h ^ flip)))
    return pairs


def local(queries, keys, values, outputs, grad_out, lse, span_order):
    tokens, heads, depth = queries.shape
    count = lax.axis_size("ctx")
    both = ("ctx", "head")
    q = queries.reshape(tokens * heads, depth)
    do = grad_out.reshape(tokens * heads, depth)
    out = outputs.reshape(tokens * heads, depth)
    over_two = ring(count, lambda d: d - 2 if d % 2 else d + 2)
    back_two = [(b, a) for a, b in over_two]
    over_one = ring(count, lambda d: d + 1 if d % 2 else d - 1)
    mates = [(d, d ^ 1) for d in range(count)]

    kv, q, do, out = load(keys, values, q, do, out)
    kv_a = lax.ppermute(kv, both, over_two)
    kv_b = lax.ppermute(kv, both, over_one)
    x = prep(do, out, lse)

    args = (tokens, span_order, q, do, x)
    dq, g_a = far(-2, 0, *args, kv_a, None, BF16, "far_a")
    kv_cd = lax.ppermute(pack(kv, kv_b, g_a), "ctx", mates)
    got_a = lax.ppermute(g_a, both, back_two)
    dq, g_b = far(-1, 0, *args, kv_b, dq, F32, "far_b")
    dq, g_d = far(2, 1, *args, kv_cd, dq, BF16, "far_d")
    got_d = lax.ppermute(g_d, "ctx", mates)
    dq, g_low = own(own_low_kernel, span_order, q, do, x, kv, [], dq, tokens // 2, "own_low", 5)
    g_bd = add(g_b, got_d, g_low, got_a)
    got_b = lax.ppermute(g_bd, both, over_one)
    dq, g_c = far(1, 0, *args, kv_cd, dq, BF16, "far_c", g_bd, 1)
    got_c = lax.ppermute(g_c, "ctx", mates)
    dq, g_own = own(own_high_kernel, span_order, q, do, x, kv, [g_low], dq, tokens, "own_high", 1)
    keep, send = merge(g_own, got_a, got_b, got_c)
    got = lax.ppermute(send, "head", [(0, 1), (1, 0)])
    grad_q = finish(dq)
    grad_k, grad_v = last(keep, got)
    return grad_q.reshape(tokens, heads, depth), grad_k, grad_v


def solution(mesh):
    return jax.shard_map(
        local,
        mesh=mesh,
        in_specs=(
            P("ctx", "head", None),
            P("ctx", None),
            P("ctx", None),
            P("ctx", "head", None),
            P("ctx", "head", None),
            P("head", "ctx"),
            P(),
        ),
        out_specs=(P("ctx", "head", None), P(("ctx", "head"), None), P(("ctx", "head"), None)),
        check_vma=False,
    )
```

```python
import functools

import jax
import jax.numpy as jnp
from jax import lax
from jax.experimental import pallas as pl
from jax.experimental.pallas import tpu as pltpu
from jax.sharding import PartitionSpec as P

F32 = jnp.float32
BF16 = jnp.bfloat16
LOG2E = 1.4426950408889634
SUB = 512
DISTANCES = (-2, -1, 1, 2)
VMEM = pl.BlockSpec(memory_space=pltpu.VMEM)
SMEM = pl.BlockSpec(memory_space=pltpu.SMEM)


def dot(a, b, ca, cb):
    return lax.dot_general(a, b, (((ca,), (cb,)), ((), ())), preferred_element_type=F32)


def lane_ones(rows, low, high):
    lane = lax.broadcasted_iota(jnp.int32, (rows, 128), 1)
    return jnp.where((lane >= low) & (lane < high), 1.0, 0.0).astype(BF16)


def load_kernel(k_ref, v_ref, q_ref, do_ref, out_ref, kv_to, q_to, do_to, out_to, sems):
    rows = k_ref.shape[0]
    copies = [
        pltpu.make_async_copy(source, target, sems.at[i])
        for i, (source, target) in enumerate(
            [
                (k_ref, kv_to.at[pl.ds(0, rows)]),
                (v_ref, kv_to.at[pl.ds(rows, rows)]),
                (do_ref, do_to),
                (out_ref, out_to),
                (q_ref, q_to),
            ]
        )
    ]
    for copy in copies:
        copy.start()
    for copy in copies:
        copy.wait()


def load(keys, values, q, do, out):
    rows, depth = keys.shape
    wide = jax.ShapeDtypeStruct(q.shape, q.dtype)
    args = [pltpu.with_memory_space_constraint(a, pltpu.HBM) for a in (keys, values, q, do, out)]
    return pl.pallas_call(
        load_kernel,
        out_shape=[jax.ShapeDtypeStruct((2 * rows, depth), keys.dtype)] + [wide] * 3,
        in_specs=[pl.BlockSpec(memory_space=pltpu.HBM)] * 5,
        out_specs=[VMEM] * 4,
        scratch_shapes=[pltpu.SemaphoreType.DMA((5,))],
        compiler_params=pltpu.CompilerParams(vmem_limit_bytes=8 * 2**20),
        name="load",
    )(*args)


def prep_kernel(span_ref, grad_ref, out_ref, lse_ref, extra_ref, code_ref, wide):
    count = lax.axis_size("ctx")
    me = lax.axis_index("ctx")
    sign = 1 - 2 * (me % 2)
    q0, q1 = span_ref[2 * me], span_ref[2 * me + 1]
    row = lax.broadcasted_iota(jnp.int32, code_ref.shape, 0)
    codes = jnp.where(row == len(DISTANCES), jnp.where(q0 > q1, 1.0, 0.0), 0.0)
    for r, distance in enumerate(DISTANCES):
        source = (me + sign * distance + count) % count
        k0, k1 = span_ref[2 * source], span_ref[2 * source + 1]
        code = 0.0
        for bit, allowed in enumerate((k0 < q0, k0 < q1, k1 < q0, k1 < q1)):
            code = code + jnp.where(allowed, float(2**bit), 0.0)
        codes = jnp.where(row == r, code, codes)
    code_ref[...] = codes
    heads, tokens = lse_ref.shape
    depth = grad_ref.shape[1]
    lse = lse_ref[...] * float(depth**0.5)
    turned = jnp.concatenate([lse, jnp.zeros((128 - heads, tokens), F32)], axis=0).T
    for g in range(heads):
        wide[pl.ds(g, tokens, stride=heads), :] = jnp.broadcast_to(
            turned[:, g : g + 1], (tokens, 128)
        )
    delta = jnp.sum(
        grad_ref[...].astype(F32) * out_ref[...].astype(F32), axis=1, keepdims=True
    )
    lane = lax.broadcasted_iota(jnp.int32, wide.shape, 1)
    rest = jnp.where(lane < 3, wide[...], delta)
    high = rest.astype(BF16).astype(F32)
    rest = rest - high
    mid = rest.astype(BF16).astype(F32)
    low = rest - mid
    place = jnp.where(lane < 3, lane, lane - 3)
    term = jnp.where(place == 0, high, jnp.where(place == 1, mid, low))
    extra_ref[...] = jnp.where(lane < 6, -term, 0.0).astype(BF16)


def read_code(code_ref, row):
    return jnp.max(code_ref[pl.ds(row, 1), :]).astype(jnp.int32)


def prep(spans, grad_rows, out_rows, lse):
    rows, depth = grad_rows.shape
    return pl.pallas_call(
        prep_kernel,
        out_shape=[
            jax.ShapeDtypeStruct((rows, 128), BF16),
            jax.ShapeDtypeStruct((8, 128), F32),
        ],
        in_specs=[SMEM] + [VMEM] * 3,
        out_specs=[VMEM] * 2,
        scratch_shapes=[pltpu.VMEM((rows, 128), F32)],
        compiler_params=pltpu.CompilerParams(vmem_limit_bytes=16 * 2**20),
        cost_estimate=pl.CostEstimate(flops=rows * 1024, bytes_accessed=rows * 768, transcendentals=0),
        name="prep",
    )(spans, grad_rows, out_rows, lse)


def tile(q_ref, do_ref, x_ref, key, value, q_base, rows, mask=None):
    span, depth = key.shape
    exponent = float(depth**-0.5 * LOG2E)
    key_x = jnp.concatenate([key, lane_ones(span, 0, 3)], axis=1)
    value_x = jnp.concatenate([value, lane_ones(span, 3, 6)], axis=1)

    def front(i):
        at = pl.ds(pl.multiple_of(q_base + i * SUB, SUB), SUB)
        q, do, x = q_ref[at, :], do_ref[at, :], x_ref[at, :]
        p = jnp.exp2(dot(jnp.concatenate([q, x], axis=1), key_x, 1, 1) * exponent)
        if mask is not None:
            p = jnp.where(mask(i * SUB, SUB, span), p, 0.0)
        dp = dot(jnp.concatenate([do, x], axis=1), value_x, 1, 1)
        return at, q, do, p.astype(BF16), (p * dp).astype(BF16)

    dk, dv = None, None
    pieces = rows // SUB
    later = front(0)
    terms = []
    for i in range(pieces):
        at, q, do, p, ds = later
        if i + 1 < pieces:
            later = front(i + 1)
        yield_dq = dot(ds, key, 1, 0)
        terms.append((at, yield_dq))
        part_v, part_k = dot(do, p, 0, 0), dot(q, ds, 0, 0)
        dv = part_v if dv is None else dv + part_v
        dk = part_k if dk is None else dk + part_k
    return terms, dk, dv


def far_kernel(first_code, chunks, first, code_ref, q_ref, do_ref, x_ref, kv_ref, *refs):
    dq_ref, g_ref = refs if first else refs[1:]
    depth = q_ref.shape[1]
    tokens = kv_ref.shape[0] // (2 * chunks)
    span = tokens // 2
    half = q_ref.shape[0] // 2

    def run(base, rows, at, keys, k_rows, v_rows, lanes, store=False):
        key, value = kv_ref[pl.ds(at, keys), :], kv_ref[pl.ds(at + tokens, keys), :]
        terms, dk, dv = tile(q_ref, do_ref, x_ref, key, value, base, rows)
        for rows_at, term in terms:
            dq_ref[rows_at, :] = term if store else dq_ref[rows_at, :] + term
        g_ref[k_rows, lanes] = dk.astype(g_ref.dtype)
        g_ref[v_rows, lanes] = dv.astype(g_ref.dtype)

    def block(chunk, carry):
        code = read_code(code_ref, first_code + chunk)
        first_row = pl.multiple_of(chunk * 2 * tokens, 2 * tokens)
        k_rows = pl.ds(pl.multiple_of(chunk * 2 * depth, depth), depth)
        v_rows = pl.ds(pl.multiple_of(chunk * 2 * depth + depth, depth), depth)
        every = code == 15

        @pl.when(every)
        def _():
            run(0, 2 * half, first_row, tokens, k_rows, v_rows, pl.ds(0, tokens), store=first)

        def one_span(j, carry):
            bits = jnp.where(j == 0, code, code // 4)
            at = pl.multiple_of(first_row + j * span, span)
            lanes = pl.ds(pl.multiple_of(j * span, span), span)
            a0, a1 = bits % 2 == 1, (bits // 2) % 2 == 1

            @pl.when(a0 & a1)
            def _():
                run(0, 2 * half, at, span, k_rows, v_rows, lanes)

            @pl.when(a0 != a1)
            def _():
                run(jnp.where(a1, half, 0), half, at, span, k_rows, v_rows, lanes)

            @pl.when(~(a0 | a1))
            def _():
                g_ref[k_rows, lanes] = jnp.zeros((depth, span), g_ref.dtype)
                g_ref[v_rows, lanes] = jnp.zeros((depth, span), g_ref.dtype)

            return carry

        @pl.when(~every)
        def _():
            if first:
                dq_ref[...] = jnp.zeros_like(dq_ref)
            lax.fori_loop(0, 2, one_span, 0)

        return carry

    if chunks == 1:
        block(0, 0)
    else:
        lax.fori_loop(0, chunks, block, 0)


def far(first_code, chunks, codes, q, do, x, kv, dq, dtype, name):
    rows, depth = q.shape
    tokens = kv.shape[0] // (2 * chunks)
    args = [codes, q, do, x, kv] + ([] if dq is None else [dq])
    return pl.pallas_call(
        functools.partial(far_kernel, first_code, chunks, dq is None),
        out_shape=[
            jax.ShapeDtypeStruct((rows, depth), F32),
            jax.ShapeDtypeStruct((chunks * 2 * depth, tokens), dtype),
        ],
        in_specs=[VMEM] * len(args),
        out_specs=[VMEM, VMEM],
        input_output_aliases={} if dq is None else {5: 0},
        compiler_params=pltpu.CompilerParams(vmem_limit_bytes=24 * 2**20),
        cost_estimate=pl.CostEstimate(
            flops=chunks * 10 * rows * tokens * depth,
            bytes_accessed=chunks * 2**20,
            transcendentals=chunks * rows * tokens,
        ),
        name=name,
    )(*args)


def own_low_kernel(code_ref, q_ref, do_ref, x_ref, kv_ref, _, dq_ref, g_ref):
    depth = q_ref.shape[1]
    tokens = kv_ref.shape[0] // 2
    span, half = tokens // 2, q_ref.shape[0] // 2
    heads = half // span
    low = read_code(code_ref, len(DISTANCES))

    def causal(base, rows, keys):
        row = lax.broadcasted_iota(jnp.int32, (rows, keys), 0)
        return heads * lax.broadcasted_iota(jnp.int32, (rows, keys), 1) - row <= base

    at = pl.multiple_of(low * span, span)
    key, value = kv_ref[pl.ds(at, span), :], kv_ref[pl.ds(at + tokens, span), :]
    terms, dk, dv = tile(q_ref, do_ref, x_ref, key, value, low * half, half, causal)
    for rows_at, term in terms:
        dq_ref[rows_at, :] += term
    g_ref[0:depth, :] = dk
    g_ref[depth : 2 * depth, :] = dv


def own_high_kernel(code_ref, q_ref, do_ref, x_ref, kv_ref, g_low_ref, _, dq_ref, g_ref):
    depth = q_ref.shape[1]
    tokens = kv_ref.shape[0] // 2
    span, half = tokens // 2, q_ref.shape[0] // 2
    heads = half // span
    low = read_code(code_ref, len(DISTANCES))

    def causal(base, rows, keys):
        row = lax.broadcasted_iota(jnp.int32, (rows, keys), 0)
        slot = lax.broadcasted_iota(jnp.int32, (1, keys), 1)
        own = (slot >= span) == (low == 0)
        return jnp.where(own, heads * (slot & (span - 1)), -1) - row <= base

    terms, dk, dv = tile(
        q_ref, do_ref, x_ref, kv_ref[0:tokens, :], kv_ref[tokens : 2 * tokens, :],
        (1 - low) * half, half, causal,
    )
    for rows_at, term in terms:
        dq_ref[rows_at, :] += term
    g_ref[0:depth, :] = dk
    g_ref[depth : 2 * depth, :] = dv
    lanes = pl.ds(pl.multiple_of(low * span, span), span)
    g_ref[:, lanes] += g_low_ref[...]


def own(kernel, codes, q, do, x, kv, extra, dq, keys, name):
    rows, depth = q.shape
    args = [codes, q, do, x, kv] + extra + [dq]
    return pl.pallas_call(
        kernel,
        out_shape=[
            jax.ShapeDtypeStruct((rows, depth), F32),
            jax.ShapeDtypeStruct((2 * depth, keys), F32),
        ],
        in_specs=[VMEM] * len(args),
        out_specs=[VMEM, VMEM],
        input_output_aliases={len(args) - 1: 0},
        compiler_params=pltpu.CompilerParams(vmem_limit_bytes=24 * 2**20),
        cost_estimate=pl.CostEstimate(
            flops=5 * rows * keys * depth, bytes_accessed=2**20, transcendentals=rows * keys // 2
        ),
        name=name,
    )(*args)


def finish_kernel(dq_ref, o_ref):
    o_ref[...] = (dq_ref[...] * float(dq_ref.shape[1] ** -0.5)).astype(BF16)


def finish(dq):
    return pl.pallas_call(
        finish_kernel,
        out_shape=jax.ShapeDtypeStruct(dq.shape, BF16),
        in_specs=[VMEM],
        out_specs=VMEM,
        compiler_params=pltpu.CompilerParams(vmem_limit_bytes=8 * 2**20),
        cost_estimate=pl.CostEstimate(flops=dq.size, bytes_accessed=6 * dq.size, transcendentals=0),
        name="finish",
    )(dq)


def add_kernel(a_ref, b_ref, o_ref):
    rows = o_ref.shape[0]
    o_ref[...] = (a_ref[...] + b_ref[pl.ds(rows, rows), :].astype(F32)).astype(BF16)


def add(a, b):
    return pl.pallas_call(
        add_kernel,
        out_shape=jax.ShapeDtypeStruct(a.shape, BF16),
        in_specs=[VMEM, VMEM],
        out_specs=VMEM,
        compiler_params=pltpu.CompilerParams(vmem_limit_bytes=8 * 2**20),
        name="add",
    )(a, b)


def merge_kernel(own_ref, a_ref, b_ref, c_ref, keep_ref, send_ref):
    rows, tokens = own_ref.shape
    half = tokens // 2
    head = lax.axis_index("head")

    def part(index):
        lanes = pl.ds(pl.multiple_of(index * half, half), half)
        return (
            own_ref[:, lanes]
            + a_ref[:, lanes].astype(F32)
            + b_ref[:, lanes].astype(F32)
            + c_ref[0:rows, lanes].astype(F32)
        )

    send_ref[...] = part(1 - head).astype(BF16)
    keep_ref[...] = part(head)


def merge(g, a, b, c):
    rows, tokens = g.shape
    return pl.pallas_call(
        merge_kernel,
        out_shape=[
            jax.ShapeDtypeStruct((rows, tokens // 2), F32),
            jax.ShapeDtypeStruct((rows, tokens // 2), BF16),
        ],
        in_specs=[VMEM] * 4,
        out_specs=[VMEM, VMEM],
        compiler_params=pltpu.CompilerParams(vmem_limit_bytes=8 * 2**20),
        name="merge",
    )(g, a, b, c)


def last_kernel(keep_ref, got_ref, dk_ref, dv_ref):
    total = keep_ref[...] + got_ref[1 - lax.axis_index("head")].astype(F32)
    depth = total.shape[0] // 2
    dk_ref[...] = (total[:depth].T * float(depth**-0.5)).astype(BF16)
    dv_ref[...] = total[depth:].T.astype(BF16)


def last(keep, got):
    rows, tokens = keep.shape
    shape = jax.ShapeDtypeStruct((tokens, rows // 2), BF16)
    return pl.pallas_call(
        last_kernel,
        out_shape=[shape, shape],
        in_specs=[VMEM, VMEM],
        out_specs=[VMEM, VMEM],
        compiler_params=pltpu.CompilerParams(vmem_limit_bytes=8 * 2**20),
        name="last",
    )(keep, got)


def pack_kernel(a_ref, b_ref, _, o_ref):
    rows = a_ref.shape[0]
    o_ref[0:rows, :] = a_ref[...]
    o_ref[rows : 2 * rows, :] = b_ref[...]


def pack(a, b, after):
    rows, depth = a.shape
    return pl.pallas_call(
        pack_kernel,
        out_shape=jax.ShapeDtypeStruct((2 * rows, depth), a.dtype),
        in_specs=[VMEM, VMEM, pl.BlockSpec(memory_space=pl.ANY)],
        out_specs=VMEM,
        compiler_params=pltpu.CompilerParams(vmem_limit_bytes=8 * 2**20),
        name="pack",
    )(a, b, after)


def ring(count, move):
    pairs = []
    for d in range(count):
        target = move(d)
        flip = 0 if 0 <= target < count else 1
        for h in range(2):
            pairs.append((2 * d + h, 2 * (target % count) + (h ^ flip)))
    return pairs


def local(queries, keys, values, outputs, grad_out, lse, span_order):
    tokens, heads, depth = queries.shape
    count = lax.axis_size("ctx")
    both = ("ctx", "head")
    q = queries.reshape(tokens * heads, depth)
    do = grad_out.reshape(tokens * heads, depth)
    out = outputs.reshape(tokens * heads, depth)
    over_two = ring(count, lambda d: d - 2 if d % 2 else d + 2)
    back_two = [(b, a) for a, b in over_two]
    over_one = ring(count, lambda d: d + 1 if d % 2 else d - 1)
    mates = [(d, d ^ 1) for d in range(count)]

    kv, q, do, out = load(keys, values, q, do, out)
    kv_a = lax.ppermute(kv, both, over_two)
    kv_b = lax.ppermute(kv, both, over_one)
    x, codes = prep(span_order, do, out, lse)

    dq, g_a = far(0, 1, codes, q, do, x, kv_a, None, BF16, "far_a")
    kv_cd = lax.ppermute(pack(kv, kv_b, g_a), "ctx", mates)
    got_a = lax.ppermute(g_a, both, back_two)
    dq, g_b = far(1, 1, codes, q, do, x, kv_b, dq, F32, "far_b")
    dq, g_cd = far(2, 2, codes, q, do, x, kv_cd, dq, BF16, "far_cd")
    got_cd = lax.ppermute(g_cd, "ctx", mates)
    span = tokens // 2
    dq, g_low = own(own_low_kernel, codes, q, do, x, kv, [], dq, span, "own_low")
    got_b = lax.ppermute(add(g_b, got_cd), both, over_one)
    dq, g_own = own(own_high_kernel, codes, q, do, x, kv, [g_low], dq, tokens, "own_high")
    keep, send = merge(g_own, got_a, got_b, got_cd)
    got = lax.all_gather(send, "head")
    grad_q = finish(dq)
    grad_k, grad_v = last(keep, got)
    return grad_q.reshape(tokens, heads, depth), grad_k, grad_v


def solution(mesh):
    return jax.shard_map(
        local,
        mesh=mesh,
        in_specs=(
            P("ctx", "head", None),
            P("ctx", None),
            P("ctx", None),
            P("ctx", "head", None),
            P("ctx", "head", None),
            P("head", "ctx"),
            P(),
        ),
        out_specs=(P("ctx", "head", None), P(("ctx", "head"), None), P(("ctx", "head"), None)),
        check_vma=False,
    )
```

```python
import functools

import jax
import jax.numpy as jnp
from jax import lax
from jax.experimental import pallas as pl
from jax.experimental.pallas import tpu as pltpu
from jax.sharding import PartitionSpec as P

F32 = jnp.float32
BF16 = jnp.bfloat16
LOG2E = 1.4426950408889634
SUB = 512
LOW = 4
VMEM = pl.BlockSpec(memory_space=pltpu.VMEM)
SMEM = pl.BlockSpec(memory_space=pltpu.SMEM)


def dot(a, b, ca, cb):
    return lax.dot_general(a, b, (((ca,), (cb,)), ((), ())), preferred_element_type=F32)


def lane_ones(rows, low, high):
    lane = lax.broadcasted_iota(jnp.int32, (rows, 128), 1)
    return jnp.where((lane >= low) & (lane < high), 1.0, 0.0).astype(BF16)


def load_kernel(k_ref, v_ref, q_ref, do_ref, out_ref, kv_to, rows_to, out_to, sems):
    tokens, rows = k_ref.shape[0], q_ref.shape[0]
    copies = [
        pltpu.make_async_copy(source, target, sems.at[i])
        for i, (source, target) in enumerate(
            [
                (k_ref, kv_to.at[pl.ds(0, tokens)]),
                (v_ref, kv_to.at[pl.ds(tokens, tokens)]),
                (do_ref, rows_to.at[pl.ds(rows, rows)]),
                (out_ref, out_to),
                (q_ref, rows_to.at[pl.ds(0, rows)]),
            ]
        )
    ]
    for copy in copies:
        copy.start()
    for copy in copies:
        copy.wait()


def load(keys, values, q, do, out):
    tokens, depth = keys.shape
    rows = q.shape[0]
    args = [pltpu.with_memory_space_constraint(a, pltpu.HBM) for a in (keys, values, q, do, out)]
    return pl.pallas_call(
        load_kernel,
        out_shape=[
            jax.ShapeDtypeStruct((2 * tokens, depth), BF16),
            jax.ShapeDtypeStruct((3 * rows, depth), BF16),
            jax.ShapeDtypeStruct((rows, depth), BF16),
        ],
        in_specs=[pl.BlockSpec(memory_space=pltpu.HBM)] * 5,
        out_specs=[VMEM] * 3,
        scratch_shapes=[pltpu.SemaphoreType.DMA((5,))],
        compiler_params=pltpu.CompilerParams(vmem_limit_bytes=8 * 2**20),
        name="load",
    )(*args)


def prep_kernel(span_ref, rows_in_ref, out_ref, lse_ref, rows_ref, code_ref, wide):
    count = lax.axis_size("ctx")
    me = lax.axis_index("ctx")
    sign = 1 - 2 * (me % 2)
    mate, near, far = me + sign, (me - sign + count) % count, (me - 2 * sign + count) % count
    row = lax.broadcasted_iota(jnp.int32, code_ref.shape, 0)
    later = span_ref[2 * me] > span_ref[2 * me + 1]
    codes = jnp.where(row == LOW, jnp.where(later, 1.0, 0.0), 0.0)
    for r, (query, source) in enumerate(((me, far), (me, near), (mate, near), (mate, me))):
        q0, q1 = span_ref[2 * query], span_ref[2 * query + 1]
        k0, k1 = span_ref[2 * source], span_ref[2 * source + 1]
        code = 0.0
        for bit, allowed in enumerate((k0 < q0, k0 < q1, k1 < q0, k1 < q1)):
            code = code + jnp.where(allowed, float(2**bit), 0.0)
        codes = jnp.where(row == r, code, codes)
    code_ref[...] = codes
    rows = out_ref.shape[0]
    heads, tokens = lse_ref.shape
    depth = out_ref.shape[1]
    lse = lse_ref[...] * float(depth**0.5)
    turned = jnp.concatenate([lse, jnp.zeros((128 - heads, tokens), F32)], axis=0).T
    for g in range(heads):
        wide[pl.ds(g, tokens, stride=heads), :] = jnp.broadcast_to(
            turned[:, g : g + 1], (tokens, 128)
        )
    delta = jnp.sum(
        rows_in_ref[rows : 2 * rows, :].astype(F32) * out_ref[...].astype(F32), axis=1, keepdims=True
    )
    lane = lax.broadcasted_iota(jnp.int32, wide.shape, 1)
    rest = jnp.where(lane < 3, wide[...], delta)
    high = rest.astype(BF16).astype(F32)
    rest = rest - high
    mid = rest.astype(BF16).astype(F32)
    low = rest - mid
    place = jnp.where(lane < 3, lane, lane - 3)
    term = jnp.where(place == 0, high, jnp.where(place == 1, mid, low))
    rows_ref[2 * rows : 3 * rows, :] = jnp.where(lane < 6, -term, 0.0).astype(BF16)


def read_code(code_ref, row):
    return jnp.max(code_ref[pl.ds(row, 1), :]).astype(jnp.int32)


def prep(spans, q_rows, out_rows, lse):
    rows = out_rows.shape[0]
    return pl.pallas_call(
        prep_kernel,
        out_shape=[
            jax.ShapeDtypeStruct(q_rows.shape, BF16),
            jax.ShapeDtypeStruct((8, 128), F32),
        ],
        in_specs=[SMEM] + [VMEM] * 3,
        out_specs=[VMEM] * 2,
        input_output_aliases={1: 0},
        scratch_shapes=[pltpu.VMEM((rows, 128), F32)],
        compiler_params=pltpu.CompilerParams(vmem_limit_bytes=16 * 2**20),
        cost_estimate=pl.CostEstimate(flops=rows * 1024, bytes_accessed=rows * 768, transcendentals=0),
        name="prep",
    )(spans, q_rows, out_rows, lse)


def tile(rows_ref, key, value, q_base, rows, mask=None):
    span, depth = key.shape
    count = rows_ref.shape[0] // 3
    exponent = float(depth**-0.5 * LOG2E)
    key_x = jnp.concatenate([key, lane_ones(span, 0, 3)], axis=1)
    value_x = jnp.concatenate([value, lane_ones(span, 3, 6)], axis=1)

    def front(i):
        first = pl.multiple_of(q_base + i * SUB, SUB)
        at = pl.ds(first, SUB)
        q, do, x = (rows_ref[pl.ds(first + part * count, SUB), :] for part in range(3))
        p = jnp.exp2(dot(jnp.concatenate([q, x], axis=1), key_x, 1, 1) * exponent)
        if mask is not None:
            p = jnp.where(mask(i * SUB, SUB, span), p, 0.0)
        dp = dot(jnp.concatenate([do, x], axis=1), value_x, 1, 1)
        return at, q, do, p.astype(BF16), (p * dp).astype(BF16)

    dk, dv = None, None
    pieces = rows // SUB
    later = front(0)
    terms = []
    for i in range(pieces):
        at, q, do, p, ds = later
        if i + 1 < pieces:
            later = front(i + 1)
        yield_dq = dot(ds, key, 1, 0)
        terms.append((at, yield_dq))
        part_v, part_k = dot(do, p, 0, 0), dot(q, ds, 0, 0)
        dv = part_v if dv is None else dv + part_v
        dk = part_k if dk is None else dk + part_k
    return terms, dk, dv


def far_kernel(row, has_dq, has_g, has_low, code_ref, rows_ref, kv_ref, *refs):
    refs = list(refs)
    dq_in = refs.pop(0) if has_dq else None
    g_in = refs.pop(0) if has_g else None
    low_ref = refs.pop() if has_low else None
    dq_ref, g_ref = refs[-2:]
    depth = kv_ref.shape[1]
    tokens = kv_ref.shape[0] // 2
    span = tokens // 2
    half = rows_ref.shape[0] // 6
    code = read_code(code_ref, row)
    every = code == 15

    def put(rows, lanes, value):
        if has_g:
            value = value + g_in[rows, lanes]
        g_ref[rows, lanes] = value.astype(g_ref.dtype)

    def run(base, count, at, keys, lanes, store=False):
        key, value = kv_ref[pl.ds(at, keys), :], kv_ref[pl.ds(at + tokens, keys), :]
        terms, dk, dv = tile(rows_ref, key, value, base, count)
        for rows_at, term in terms:
            dq_ref[rows_at, :] = term if store else dq_ref[rows_at, :] + term
        put(pl.ds(0, depth), lanes, dk)
        put(pl.ds(depth, depth), lanes, dv)

    @pl.when(every)
    def _():
        run(0, 2 * half, 0, tokens, pl.ds(0, tokens), store=not has_dq)

    def one_span(j, carry):
        bits = jnp.where(j == 0, code, code // 4)
        at = pl.multiple_of(j * span, span)
        lanes = pl.ds(at, span)
        a0, a1 = bits % 2 == 1, (bits // 2) % 2 == 1

        @pl.when(a0 & a1)
        def _():
            run(0, 2 * half, at, span, lanes)

        @pl.when(a0 != a1)
        def _():
            run(jnp.where(a1, half, 0), half, at, span, lanes)

        @pl.when(~(a0 | a1))
        def _():
            put(pl.ds(0, 2 * depth), lanes, jnp.zeros((2 * depth, span), F32))

        return carry

    @pl.when(~every)
    def _():
        if not has_dq:
            dq_ref[...] = jnp.zeros_like(dq_ref)
        lax.fori_loop(0, 2, one_span, 0)

    if has_low:
        low_ref[...] = dq_ref[...].astype(BF16)


def far(row, codes, q_rows, kv, name, dq=None, g=None, dtype=F32, low=False, weight=10):
    rows, depth = q_rows.shape[0] // 3, q_rows.shape[1]
    tokens = kv.shape[0] // 2
    args = [codes, q_rows, kv] + [a for a in (dq, g) if a is not None]
    wide = jax.ShapeDtypeStruct((rows, depth), F32)
    return pl.pallas_call(
        functools.partial(far_kernel, row, dq is not None, g is not None, low),
        out_shape=[wide, jax.ShapeDtypeStruct((2 * depth, tokens), dtype)]
        + ([jax.ShapeDtypeStruct((rows, depth), BF16)] if low else []),
        in_specs=[VMEM] * len(args),
        out_specs=[VMEM] * (3 if low else 2),
        input_output_aliases={} if dq is None else {3: 0},
        compiler_params=pltpu.CompilerParams(vmem_limit_bytes=24 * 2**20),
        cost_estimate=pl.CostEstimate(
            flops=weight * rows * tokens * depth,
            bytes_accessed=2**16,
            transcendentals=weight * rows * tokens // 10,
        ),
        name=name,
    )(*args)


def own_low_kernel(code_ref, rows_ref, kv_ref, _, dq_ref, g_ref):
    depth = kv_ref.shape[1]
    tokens = kv_ref.shape[0] // 2
    span, half = tokens // 2, rows_ref.shape[0] // 6
    heads = half // span
    low = read_code(code_ref, LOW)

    def causal(base, rows, keys):
        row = lax.broadcasted_iota(jnp.int32, (rows, keys), 0)
        return heads * lax.broadcasted_iota(jnp.int32, (rows, keys), 1) - row <= base

    at = pl.multiple_of(low * span, span)
    key, value = kv_ref[pl.ds(at, span), :], kv_ref[pl.ds(at + tokens, span), :]
    terms, dk, dv = tile(rows_ref, key, value, low * half, half, causal)
    for rows_at, term in terms:
        dq_ref[rows_at, :] += term
    g_ref[0:depth, :] = dk
    g_ref[depth : 2 * depth, :] = dv


def own_high_kernel(code_ref, rows_ref, kv_ref, g_low_ref, _, dq_ref, g_ref):
    depth = kv_ref.shape[1]
    tokens = kv_ref.shape[0] // 2
    span, half = tokens // 2, rows_ref.shape[0] // 6
    heads = half // span
    low = read_code(code_ref, LOW)

    def causal(base, rows, keys):
        row = lax.broadcasted_iota(jnp.int32, (rows, keys), 0)
        slot = lax.broadcasted_iota(jnp.int32, (1, keys), 1)
        own = (slot >= span) == (low == 0)
        return jnp.where(own, heads * (slot & (span - 1)), -1) - row <= base

    terms, dk, dv = tile(
        rows_ref, kv_ref[0:tokens, :], kv_ref[tokens : 2 * tokens, :],
        (1 - low) * half, half, causal,
    )
    for rows_at, term in terms:
        dq_ref[rows_at, :] += term
    g_ref[0:depth, :] = dk
    g_ref[depth : 2 * depth, :] = dv
    lanes = pl.ds(pl.multiple_of(low * span, span), span)
    g_ref[:, lanes] += g_low_ref[...]


def own(kernel, codes, q_rows, kv, extra, dq, keys, name):
    rows, depth = dq.shape
    args = [codes, q_rows, kv] + extra + [dq]
    return pl.pallas_call(
        kernel,
        out_shape=[
            jax.ShapeDtypeStruct((rows, depth), F32),
            jax.ShapeDtypeStruct((2 * depth, keys), F32),
        ],
        in_specs=[VMEM] * len(args),
        out_specs=[VMEM, VMEM],
        input_output_aliases={len(args) - 1: 0},
        compiler_params=pltpu.CompilerParams(vmem_limit_bytes=24 * 2**20),
        cost_estimate=pl.CostEstimate(
            flops=rows * keys * depth // 10, bytes_accessed=2**16, transcendentals=rows * keys // 100
        ),
        name=name,
    )(*args)


def finish_kernel(dq_ref, mate_ref, o_ref):
    total = dq_ref[...] + mate_ref[...].astype(F32)
    o_ref[...] = (total * float(dq_ref.shape[1] ** -0.5)).astype(BF16)


def finish(dq, mate):
    return pl.pallas_call(
        finish_kernel,
        out_shape=jax.ShapeDtypeStruct(dq.shape, BF16),
        in_specs=[VMEM, VMEM],
        out_specs=VMEM,
        compiler_params=pltpu.CompilerParams(vmem_limit_bytes=8 * 2**20),
        cost_estimate=pl.CostEstimate(flops=dq.size, bytes_accessed=6 * dq.size, transcendentals=0),
        name="finish",
    )(dq, mate)


def merge_kernel(own_ref, a_ref, b_ref, c_ref, _, keep_ref, send_ref):
    rows, tokens = own_ref.shape
    half = tokens // 2
    head = lax.axis_index("head")

    def part(index):
        lanes = pl.ds(pl.multiple_of(index * half, half), half)
        return (
            own_ref[:, lanes]
            + a_ref[:, lanes].astype(F32)
            + b_ref[:, lanes].astype(F32)
            + c_ref[:, lanes]
        )

    send_ref[...] = part(1 - head).astype(BF16)
    keep_ref[...] = part(head)


def merge(g, a, b, c, after):
    rows, tokens = g.shape
    return pl.pallas_call(
        merge_kernel,
        out_shape=[
            jax.ShapeDtypeStruct((rows, tokens // 2), F32),
            jax.ShapeDtypeStruct((rows, tokens // 2), BF16),
        ],
        in_specs=[VMEM] * 4 + [pl.BlockSpec(memory_space=pl.ANY)],
        out_specs=[VMEM, VMEM],
        compiler_params=pltpu.CompilerParams(vmem_limit_bytes=8 * 2**20),
        name="merge",
    )(g, a, b, c, after)


def last_kernel(keep_ref, got_ref, dk_ref, dv_ref):
    total = keep_ref[...] + got_ref[1 - lax.axis_index("head")].astype(F32)
    depth = total.shape[0] // 2
    dk_ref[...] = (total[:depth].T * float(depth**-0.5)).astype(BF16)
    dv_ref[...] = total[depth:].T.astype(BF16)


def last(keep, got):
    rows, tokens = keep.shape
    shape = jax.ShapeDtypeStruct((tokens, rows // 2), BF16)
    return pl.pallas_call(
        last_kernel,
        out_shape=[shape, shape],
        in_specs=[VMEM, VMEM],
        out_specs=[VMEM, VMEM],
        compiler_params=pltpu.CompilerParams(vmem_limit_bytes=8 * 2**20),
        name="last",
    )(keep, got)


def ring(count, move):
    pairs = []
    for d in range(count):
        target = move(d)
        flip = 0 if 0 <= target < count else 1
        for h in range(2):
            pairs.append((2 * d + h, 2 * (target % count) + (h ^ flip)))
    return pairs


def local(queries, keys, values, outputs, grad_out, lse, span_order):
    tokens, heads, depth = queries.shape
    count = lax.axis_size("ctx")
    both = ("ctx", "head")
    q = queries.reshape(tokens * heads, depth)
    do = grad_out.reshape(tokens * heads, depth)
    out = outputs.reshape(tokens * heads, depth)
    over_two = ring(count, lambda d: d - 2 if d % 2 else d + 2)
    back_two = [(b, a) for a, b in over_two]
    over_one = ring(count, lambda d: d + 1 if d % 2 else d - 1)
    mates = [(d, d ^ 1) for d in range(count)]

    kv, q_rows, out = load(keys, values, q, do, out)
    kv_a = lax.ppermute(kv, both, over_two)
    kv_b = lax.ppermute(kv, both, over_one)
    q_rows, codes = prep(span_order, q_rows, out, lse)
    mate_rows = lax.ppermute(q_rows, "ctx", mates)

    dq, g_a = far(0, codes, q_rows, kv_a, "far_a", dtype=BF16)
    got_a = lax.ppermute(g_a, both, back_two)
    dq, g_b = far(1, codes, q_rows, kv_b, "far_b", dq=dq, weight=1000)
    dq_mate, g_mate = far(3, codes, mate_rows, kv, "own_mate")
    _, g_b, dq_low = far(
        2, codes, mate_rows, kv_b, "far_b_mate", dq=dq_mate, g=g_b, dtype=BF16, low=True
    )
    got_b = lax.ppermute(g_b, both, over_one)
    got_dq = lax.ppermute(dq_low, "ctx", mates)
    dq, g_low = own(own_low_kernel, codes, q_rows, kv, [], dq, tokens // 2, "own_low")
    dq, g_own = own(own_high_kernel, codes, q_rows, kv, [g_low], dq, tokens, "own_high")
    grad_q = finish(dq, got_dq)
    keep, send = merge(g_own, got_a, got_b, g_mate, grad_q)
    got = lax.all_gather(send, "head")
    grad_k, grad_v = last(keep, got)
    return grad_q.reshape(tokens, heads, depth), grad_k, grad_v


def solution(mesh):
    return jax.shard_map(
        local,
        mesh=mesh,
        in_specs=(
            P("ctx", "head", None),
            P("ctx", None),
            P("ctx", None),
            P("ctx", "head", None),
            P("ctx", "head", None),
            P("head", "ctx"),
            P(),
        ),
        out_specs=(P("ctx", "head", None), P(("ctx", "head"), None), P(("ctx", "head"), None)),
        check_vma=False,
    )
```

```python
import functools

import jax
import jax.numpy as jnp
from jax import lax
from jax.experimental import pallas as pl
from jax.experimental.pallas import tpu as pltpu
from jax.sharding import PartitionSpec as P

F32 = jnp.float32
BF16 = jnp.bfloat16
LOG2E = 1.4426950408889634
SUB = 512
LOW = 4
VMEM = pl.BlockSpec(memory_space=pltpu.VMEM)
SMEM = pl.BlockSpec(memory_space=pltpu.SMEM)


def dot(a, b, ca, cb):
    return lax.dot_general(a, b, (((ca,), (cb,)), ((), ())), preferred_element_type=F32)


def lane_ones(rows, low, high):
    lane = lax.broadcasted_iota(jnp.int32, (rows, 128), 1)
    return jnp.where((lane >= low) & (lane < high), 1.0, 0.0).astype(BF16)


def load_kernel(k_ref, v_ref, q_ref, do_ref, out_ref, kv_to, rows_to, out_to, sems):
    tokens, rows = k_ref.shape[0], q_ref.shape[0]
    copies = [
        pltpu.make_async_copy(source, target, sems.at[i])
        for i, (source, target) in enumerate(
            [
                (k_ref, kv_to.at[pl.ds(0, tokens)]),
                (v_ref, kv_to.at[pl.ds(tokens, tokens)]),
                (do_ref, rows_to.at[pl.ds(rows, rows)]),
                (out_ref, out_to),
                (q_ref, rows_to.at[pl.ds(0, rows)]),
            ]
        )
    ]
    for copy in copies:
        copy.start()
    for copy in copies:
        copy.wait()


def load(keys, values, q, do, out):
    tokens, depth = keys.shape
    rows = q.shape[0]
    args = [pltpu.with_memory_space_constraint(a, pltpu.HBM) for a in (keys, values, q, do, out)]
    return pl.pallas_call(
        load_kernel,
        out_shape=[
            jax.ShapeDtypeStruct((2 * tokens, depth), BF16),
            jax.ShapeDtypeStruct((3 * rows, depth), BF16),
            jax.ShapeDtypeStruct((rows, depth), BF16),
        ],
        in_specs=[pl.BlockSpec(memory_space=pltpu.HBM)] * 5,
        out_specs=[VMEM] * 3,
        scratch_shapes=[pltpu.SemaphoreType.DMA((5,))],
        compiler_params=pltpu.CompilerParams(vmem_limit_bytes=8 * 2**20),
        name="load",
    )(*args)


def prep_kernel(span_ref, rows_in_ref, out_ref, lse_ref, rows_ref, code_ref, wide):
    count = lax.axis_size("ctx")
    me = lax.axis_index("ctx")
    sign = 1 - 2 * (me % 2)
    mate, near, far = me + sign, (me - sign + count) % count, (me - 2 * sign + count) % count
    row = lax.broadcasted_iota(jnp.int32, code_ref.shape, 0)
    later = span_ref[2 * me] > span_ref[2 * me + 1]
    codes = jnp.where(row == LOW, jnp.where(later, 1.0, 0.0), 0.0)
    for r, (query, source) in enumerate(((me, far), (me, near), (mate, near), (mate, me))):
        q0, q1 = span_ref[2 * query], span_ref[2 * query + 1]
        k0, k1 = span_ref[2 * source], span_ref[2 * source + 1]
        code = 0.0
        for bit, allowed in enumerate((k0 < q0, k0 < q1, k1 < q0, k1 < q1)):
            code = code + jnp.where(allowed, float(2**bit), 0.0)
        codes = jnp.where(row == r, code, codes)
    code_ref[...] = codes
    rows = out_ref.shape[0]
    heads, tokens = lse_ref.shape
    depth = out_ref.shape[1]
    lse = lse_ref[...] * float(depth**0.5)
    turned = jnp.concatenate([lse, jnp.zeros((128 - heads, tokens), F32)], axis=0).T
    for g in range(heads):
        wide[pl.ds(g, tokens, stride=heads), :] = jnp.broadcast_to(
            turned[:, g : g + 1], (tokens, 128)
        )
    delta = jnp.sum(
        rows_in_ref[rows : 2 * rows, :].astype(F32) * out_ref[...].astype(F32), axis=1, keepdims=True
    )
    lane = lax.broadcasted_iota(jnp.int32, wide.shape, 1)
    rest = jnp.where(lane < 3, wide[...], delta)
    high = rest.astype(BF16).astype(F32)
    rest = rest - high
    mid = rest.astype(BF16).astype(F32)
    low = rest - mid
    place = jnp.where(lane < 3, lane, lane - 3)
    term = jnp.where(place == 0, high, jnp.where(place == 1, mid, low))
    rows_ref[2 * rows : 3 * rows, :] = jnp.where(lane < 6, -term, 0.0).astype(BF16)


def read_code(code_ref, row):
    return jnp.max(code_ref[pl.ds(row, 1), :]).astype(jnp.int32)


def prep(spans, q_rows, out_rows, lse):
    rows = out_rows.shape[0]
    return pl.pallas_call(
        prep_kernel,
        out_shape=[
            jax.ShapeDtypeStruct(q_rows.shape, BF16),
            jax.ShapeDtypeStruct((8, 128), F32),
        ],
        in_specs=[SMEM] + [VMEM] * 3,
        out_specs=[VMEM] * 2,
        input_output_aliases={1: 0},
        scratch_shapes=[pltpu.VMEM((rows, 128), F32)],
        compiler_params=pltpu.CompilerParams(vmem_limit_bytes=16 * 2**20),
        cost_estimate=pl.CostEstimate(flops=rows * 1024, bytes_accessed=rows * 768, transcendentals=0),
        name="prep",
    )(spans, q_rows, out_rows, lse)


def tile(rows_ref, key, value, q_base, rows, mask=None):
    span, depth = key.shape
    count = rows_ref.shape[0] // 3
    exponent = float(depth**-0.5 * LOG2E)
    key_x = jnp.concatenate([key, lane_ones(span, 0, 3)], axis=1)
    value_x = jnp.concatenate([value, lane_ones(span, 3, 6)], axis=1)

    def front(i):
        first = pl.multiple_of(q_base + i * SUB, SUB)
        at = pl.ds(first, SUB)
        q, do, x = (rows_ref[pl.ds(first + part * count, SUB), :] for part in range(3))
        p = jnp.exp2(dot(jnp.concatenate([q, x], axis=1), key_x, 1, 1) * exponent)
        if mask is not None:
            p = jnp.where(mask(i * SUB, SUB, span), p, 0.0)
        dp = dot(jnp.concatenate([do, x], axis=1), value_x, 1, 1)
        return at, q, do, p.astype(BF16), (p * dp).astype(BF16)

    dk, dv = None, None
    pieces = rows // SUB
    later = front(0)
    terms = []
    for i in range(pieces):
        at, q, do, p, ds = later
        if i + 1 < pieces:
            later = front(i + 1)
        yield_dq = dot(ds, key, 1, 0)
        terms.append((at, yield_dq))
        part_v, part_k = dot(do, p, 0, 0), dot(q, ds, 0, 0)
        dv = part_v if dv is None else dv + part_v
        dk = part_k if dk is None else dk + part_k
    return terms, dk, dv


def far_kernel(row, has_dq, has_g, has_low, code_ref, rows_ref, kv_ref, *refs):
    refs = list(refs)
    dq_in = refs.pop(0) if has_dq else None
    g_in = refs.pop(0) if has_g else None
    low_ref = refs.pop() if has_low else None
    dq_ref, g_ref = refs[-2:]
    depth = kv_ref.shape[1]
    tokens = kv_ref.shape[0] // 2
    span = tokens // 2
    half = rows_ref.shape[0] // 6
    code = read_code(code_ref, row)
    every = code == 15

    def put(rows, lanes, value):
        if has_g:
            value = value + g_in[rows, lanes]
        g_ref[rows, lanes] = value.astype(g_ref.dtype)

    def run(base, count, at, keys, lanes, store=False):
        key, value = kv_ref[pl.ds(at, keys), :], kv_ref[pl.ds(at + tokens, keys), :]
        terms, dk, dv = tile(rows_ref, key, value, base, count)
        for rows_at, term in terms:
            dq_ref[rows_at, :] = term if store else dq_ref[rows_at, :] + term
        put(pl.ds(0, depth), lanes, dk)
        put(pl.ds(depth, depth), lanes, dv)

    @pl.when(every)
    def _():
        run(0, 2 * half, 0, tokens, pl.ds(0, tokens), store=not has_dq)

    def one_span(j, carry):
        bits = jnp.where(j == 0, code, code // 4)
        at = pl.multiple_of(j * span, span)
        lanes = pl.ds(at, span)
        a0, a1 = bits % 2 == 1, (bits // 2) % 2 == 1

        @pl.when(a0 & a1)
        def _():
            run(0, 2 * half, at, span, lanes)

        @pl.when(a0 != a1)
        def _():
            run(jnp.where(a1, half, 0), half, at, span, lanes)

        @pl.when(~(a0 | a1))
        def _():
            put(pl.ds(0, 2 * depth), lanes, jnp.zeros((2 * depth, span), F32))

        return carry

    @pl.when(~every)
    def _():
        if not has_dq:
            dq_ref[...] = jnp.zeros_like(dq_ref)
        lax.fori_loop(0, 2, one_span, 0)

    if has_low:
        low_ref[...] = dq_ref[...].astype(BF16)


def far(row, codes, q_rows, kv, name, dq=None, g=None, dtype=F32, low=False, weight=10):
    rows, depth = q_rows.shape[0] // 3, q_rows.shape[1]
    tokens = kv.shape[0] // 2
    args = [codes, q_rows, kv] + [a for a in (dq, g) if a is not None]
    wide = jax.ShapeDtypeStruct((rows, depth), F32)
    return pl.pallas_call(
        functools.partial(far_kernel, row, dq is not None, g is not None, low),
        out_shape=[wide, jax.ShapeDtypeStruct((2 * depth, tokens), dtype)]
        + ([jax.ShapeDtypeStruct((rows, depth), BF16)] if low else []),
        in_specs=[VMEM] * len(args),
        out_specs=[VMEM] * (3 if low else 2),
        input_output_aliases={} if dq is None else {3: 0},
        compiler_params=pltpu.CompilerParams(vmem_limit_bytes=24 * 2**20),
        cost_estimate=pl.CostEstimate(
            flops=weight * rows * tokens * depth,
            bytes_accessed=2**16,
            transcendentals=weight * rows * tokens // 10,
        ),
        name=name,
    )(*args)


def own_low_kernel(code_ref, rows_ref, kv_ref, _, __, dq_ref, g_ref):
    depth = kv_ref.shape[1]
    tokens = kv_ref.shape[0] // 2
    span, half = tokens // 2, rows_ref.shape[0] // 6
    heads = half // span
    low = read_code(code_ref, LOW)

    def causal(base, rows, keys):
        row = lax.broadcasted_iota(jnp.int32, (rows, keys), 0)
        return heads * lax.broadcasted_iota(jnp.int32, (rows, keys), 1) - row <= base

    at = pl.multiple_of(low * span, span)
    key, value = kv_ref[pl.ds(at, span), :], kv_ref[pl.ds(at + tokens, span), :]
    terms, dk, dv = tile(rows_ref, key, value, low * half, half, causal)
    for rows_at, term in terms:
        dq_ref[rows_at, :] += term
    g_ref[0:depth, :] = dk
    g_ref[depth : 2 * depth, :] = dv


def own_high_kernel(code_ref, rows_ref, kv_ref, g_low_ref, _, dq_ref, g_ref):
    depth = kv_ref.shape[1]
    tokens = kv_ref.shape[0] // 2
    span, half = tokens // 2, rows_ref.shape[0] // 6
    heads = half // span
    low = read_code(code_ref, LOW)

    def causal(base, rows, keys):
        row = lax.broadcasted_iota(jnp.int32, (rows, keys), 0)
        slot = lax.broadcasted_iota(jnp.int32, (1, keys), 1)
        own = (slot >= span) == (low == 0)
        return jnp.where(own, heads * (slot & (span - 1)), -1) - row <= base

    terms, dk, dv = tile(
        rows_ref, kv_ref[0:tokens, :], kv_ref[tokens : 2 * tokens, :],
        (1 - low) * half, half, causal,
    )
    for rows_at, term in terms:
        dq_ref[rows_at, :] += term
    g_ref[0:depth, :] = dk
    g_ref[depth : 2 * depth, :] = dv
    lanes = pl.ds(pl.multiple_of(low * span, span), span)
    g_ref[:, lanes] += g_low_ref[...]


def own(kernel, codes, q_rows, kv, extra, dq, keys, name, weight):
    rows, depth = dq.shape
    args = [codes, q_rows, kv] + extra + [dq]
    return pl.pallas_call(
        kernel,
        out_shape=[
            jax.ShapeDtypeStruct((rows, depth), F32),
            jax.ShapeDtypeStruct((2 * depth, keys), F32),
        ],
        in_specs=[VMEM] * len(args),
        out_specs=[VMEM, VMEM],
        input_output_aliases={len(args) - 1: 0},
        compiler_params=pltpu.CompilerParams(vmem_limit_bytes=24 * 2**20),
        cost_estimate=pl.CostEstimate(
            flops=weight * rows * keys * depth // 10, bytes_accessed=2**16, transcendentals=rows * keys // 100
        ),
        name=name,
    )(*args)


def finish_kernel(dq_ref, mate_ref, o_ref):
    total = dq_ref[...] + mate_ref[...].astype(F32)
    o_ref[...] = (total * float(dq_ref.shape[1] ** -0.5)).astype(BF16)


def finish(dq, mate):
    return pl.pallas_call(
        finish_kernel,
        out_shape=jax.ShapeDtypeStruct(dq.shape, BF16),
        in_specs=[VMEM, VMEM],
        out_specs=VMEM,
        compiler_params=pltpu.CompilerParams(vmem_limit_bytes=8 * 2**20),
        cost_estimate=pl.CostEstimate(flops=dq.size, bytes_accessed=6 * dq.size, transcendentals=0),
        name="finish",
    )(dq, mate)


def merge_kernel(own_ref, a_ref, b_ref, c_ref, _, keep_ref, send_ref):
    rows, tokens = own_ref.shape
    half = tokens // 2
    head = lax.axis_index("head")

    def part(index):
        lanes = pl.ds(pl.multiple_of(index * half, half), half)
        return (
            own_ref[:, lanes]
            + a_ref[:, lanes].astype(F32)
            + b_ref[:, lanes].astype(F32)
            + c_ref[:, lanes]
        )

    send_ref[...] = part(1 - head).astype(BF16)
    keep_ref[...] = part(head)


def merge(g, a, b, c, after):
    rows, tokens = g.shape
    return pl.pallas_call(
        merge_kernel,
        out_shape=[
            jax.ShapeDtypeStruct((rows, tokens // 2), F32),
            jax.ShapeDtypeStruct((rows, tokens // 2), BF16),
        ],
        in_specs=[VMEM] * 4 + [pl.BlockSpec(memory_space=pltpu.HBM)],
        out_specs=[VMEM, VMEM],
        compiler_params=pltpu.CompilerParams(vmem_limit_bytes=8 * 2**20),
        name="merge",
    )(g, a, b, c, pltpu.with_memory_space_constraint(after, pltpu.HBM))


def last_kernel(keep_ref, got_ref, dk_ref, dv_ref):
    total = keep_ref[...] + got_ref[1 - lax.axis_index("head")].astype(F32)
    depth = total.shape[0] // 2
    dk_ref[...] = (total[:depth].T * float(depth**-0.5)).astype(BF16)
    dv_ref[...] = total[depth:].T.astype(BF16)


def last(keep, got):
    rows, tokens = keep.shape
    shape = jax.ShapeDtypeStruct((tokens, rows // 2), BF16)
    return pl.pallas_call(
        last_kernel,
        out_shape=[shape, shape],
        in_specs=[VMEM, VMEM],
        out_specs=[VMEM, VMEM],
        compiler_params=pltpu.CompilerParams(vmem_limit_bytes=8 * 2**20),
        name="last",
    )(keep, got)


def ring(count, move):
    pairs = []
    for d in range(count):
        target = move(d)
        flip = 0 if 0 <= target < count else 1
        for h in range(2):
            pairs.append((2 * d + h, 2 * (target % count) + (h ^ flip)))
    return pairs


def local(queries, keys, values, outputs, grad_out, lse, span_order):
    tokens, heads, depth = queries.shape
    count = lax.axis_size("ctx")
    both = ("ctx", "head")
    q = queries.reshape(tokens * heads, depth)
    do = grad_out.reshape(tokens * heads, depth)
    out = outputs.reshape(tokens * heads, depth)
    over_two = ring(count, lambda d: d - 2 if d % 2 else d + 2)
    back_two = [(b, a) for a, b in over_two]
    over_one = ring(count, lambda d: d + 1 if d % 2 else d - 1)
    mates = [(d, d ^ 1) for d in range(count)]

    kv, q_rows, out = load(keys, values, q, do, out)
    kv_a = lax.ppermute(kv, both, over_two)
    kv_b = lax.ppermute(kv, both, over_one)
    q_rows, codes = prep(span_order, q_rows, out, lse)
    mate_rows = lax.ppermute(q_rows, "ctx", mates)

    dq, g_a = far(0, codes, q_rows, kv_a, "far_a", dtype=BF16)
    got_a = lax.ppermute(g_a, both, back_two)
    dq, g_b = far(1, codes, q_rows, kv_b, "far_b", dq=dq, weight=1000)
    dq_mate, g_mate = far(3, codes, mate_rows, kv, "own_mate")
    _, g_b, dq_low = far(
        2, codes, mate_rows, kv_b, "far_b_mate", dq=dq_mate, g=g_b, dtype=BF16, low=True
    )
    got_b = lax.ppermute(g_b, both, over_one)
    got_dq = lax.ppermute(dq_low, "ctx", mates)
    dq, g_low = own(own_low_kernel, codes, q_rows, kv, [got_a], dq, tokens // 2, "own_low", 10000)
    dq, g_own = own(own_high_kernel, codes, q_rows, kv, [g_low], dq, tokens, "own_high", 1)
    grad_q = finish(dq, got_dq)
    keep, send = merge(g_own, got_a, got_b, g_mate, grad_q)
    got = lax.all_gather(send, "head")
    grad_k, grad_v = last(keep, got)
    return grad_q.reshape(tokens, heads, depth), grad_k, grad_v


def solution(mesh):
    return jax.shard_map(
        local,
        mesh=mesh,
        in_specs=(
            P("ctx", "head", None),
            P("ctx", None),
            P("ctx", None),
            P("ctx", "head", None),
            P("ctx", "head", None),
            P("head", "ctx"),
            P(),
        ),
        out_specs=(P("ctx", "head", None), P(("ctx", "head"), None), P(("ctx", "head"), None)),
        check_vma=False,
    )
```

```python
import functools

import jax
import jax.numpy as jnp
from jax import lax
from jax.experimental import pallas as pl
from jax.experimental.pallas import tpu as pltpu
from jax.sharding import PartitionSpec as P

F32 = jnp.float32
BF16 = jnp.bfloat16
LOG2E = 1.4426950408889634
SUB = 512
LOW = 4
VMEM = pl.BlockSpec(memory_space=pltpu.VMEM)
SMEM = pl.BlockSpec(memory_space=pltpu.SMEM)


def dot(a, b, ca, cb):
    return lax.dot_general(a, b, (((ca,), (cb,)), ((), ())), preferred_element_type=F32)


def lane_ones(rows, low, high):
    lane = lax.broadcasted_iota(jnp.int32, (rows, 128), 1)
    return jnp.where((lane >= low) & (lane < high), 1.0, 0.0).astype(BF16)


def load_kernel(
    span_from, k_ref, v_ref, q_ref, do_ref, out_ref, kv_to, rows_to, out_to, code_ref, span_ref, sems
):
    tokens, rows = k_ref.shape[0], q_ref.shape[0]
    copies = [
        pltpu.make_async_copy(source, target, sems.at[i])
        for i, (source, target) in enumerate(
            [
                (span_from, span_ref),
                (k_ref, kv_to.at[pl.ds(0, tokens)]),
                (v_ref, kv_to.at[pl.ds(tokens, tokens)]),
                (do_ref, rows_to.at[pl.ds(rows, rows)]),
                (out_ref, out_to),
                (q_ref, rows_to.at[pl.ds(0, rows)]),
            ]
        )
    ]
    for copy in copies:
        copy.start()
    copies[0].wait()
    count = lax.axis_size("ctx")
    me = lax.axis_index("ctx")
    sign = 1 - 2 * (me % 2)
    mate, near, far = me + sign, (me - sign + count) % count, (me - 2 * sign + count) % count
    row = lax.broadcasted_iota(jnp.int32, code_ref.shape, 0)
    later = span_ref[2 * me] > span_ref[2 * me + 1]
    codes = jnp.where(row == LOW, jnp.where(later, 1.0, 0.0), 0.0)
    for r, (query, source) in enumerate(((me, far), (me, near), (mate, near), (mate, me))):
        q0, q1 = span_ref[2 * query], span_ref[2 * query + 1]
        k0, k1 = span_ref[2 * source], span_ref[2 * source + 1]
        code = 0.0
        for bit, allowed in enumerate((k0 < q0, k0 < q1, k1 < q0, k1 < q1)):
            code = code + jnp.where(allowed, float(2**bit), 0.0)
        codes = jnp.where(row == r, code, codes)
    code_ref[...] = codes
    for copy in copies[1:]:
        copy.wait()


def load(spans, keys, values, q, do, out):
    tokens, depth = keys.shape
    rows = q.shape[0]
    args = [pltpu.with_memory_space_constraint(a, pltpu.HBM) for a in (spans, keys, values, q, do, out)]
    return pl.pallas_call(
        load_kernel,
        out_shape=[
            jax.ShapeDtypeStruct((2 * tokens, depth), BF16),
            jax.ShapeDtypeStruct((3 * rows, depth), BF16),
            jax.ShapeDtypeStruct((rows, depth), BF16),
            jax.ShapeDtypeStruct((8, 128), F32),
        ],
        in_specs=[pl.BlockSpec(memory_space=pltpu.HBM)] * 6,
        out_specs=[VMEM] * 4,
        scratch_shapes=[pltpu.SMEM(spans.shape, jnp.int32), pltpu.SemaphoreType.DMA((6,))],
        compiler_params=pltpu.CompilerParams(vmem_limit_bytes=8 * 2**20),
        name="load",
    )(*args)


def prep_kernel(rows_in_ref, out_ref, lse_ref, rows_ref, wide):
    rows = out_ref.shape[0]
    heads, tokens = lse_ref.shape
    depth = out_ref.shape[1]
    lse = lse_ref[...] * float(depth**0.5)
    turned = jnp.concatenate([lse, jnp.zeros((128 - heads, tokens), F32)], axis=0).T
    for g in range(heads):
        wide[pl.ds(g, tokens, stride=heads), :] = jnp.broadcast_to(
            turned[:, g : g + 1], (tokens, 128)
        )
    delta = jnp.sum(
        rows_in_ref[rows : 2 * rows, :].astype(F32) * out_ref[...].astype(F32), axis=1, keepdims=True
    )
    lane = lax.broadcasted_iota(jnp.int32, wide.shape, 1)
    rest = jnp.where(lane < 3, wide[...], delta)
    high = rest.astype(BF16).astype(F32)
    rest = rest - high
    mid = rest.astype(BF16).astype(F32)
    low = rest - mid
    place = jnp.where(lane < 3, lane, lane - 3)
    term = jnp.where(place == 0, high, jnp.where(place == 1, mid, low))
    rows_ref[2 * rows : 3 * rows, :] = jnp.where(lane < 6, -term, 0.0).astype(BF16)


def read_code(code_ref, row):
    return jnp.max(code_ref[pl.ds(row, 1), :]).astype(jnp.int32)


def prep(q_rows, out_rows, lse):
    rows = out_rows.shape[0]
    return pl.pallas_call(
        prep_kernel,
        out_shape=jax.ShapeDtypeStruct(q_rows.shape, BF16),
        in_specs=[VMEM] * 3,
        out_specs=VMEM,
        input_output_aliases={0: 0},
        scratch_shapes=[pltpu.VMEM((rows, 128), F32)],
        compiler_params=pltpu.CompilerParams(vmem_limit_bytes=16 * 2**20),
        cost_estimate=pl.CostEstimate(flops=rows * 1024, bytes_accessed=rows * 768, transcendentals=0),
        name="prep",
    )(q_rows, out_rows, lse)


def tile(rows_ref, key, value, q_base, rows, mask=None):
    span, depth = key.shape
    count = rows_ref.shape[0] // 3
    exponent = float(depth**-0.5 * LOG2E)
    key_x = jnp.concatenate([key, lane_ones(span, 0, 3)], axis=1)
    value_x = jnp.concatenate([value, lane_ones(span, 3, 6)], axis=1)

    def front(i):
        first = pl.multiple_of(q_base + i * SUB, SUB)
        at = pl.ds(first, SUB)
        q, do, x = (rows_ref[pl.ds(first + part * count, SUB), :] for part in range(3))
        p = jnp.exp2(dot(jnp.concatenate([q, x], axis=1), key_x, 1, 1) * exponent)
        if mask is not None:
            p = jnp.where(mask(i * SUB, SUB, span), p, 0.0)
        dp = dot(jnp.concatenate([do, x], axis=1), value_x, 1, 1)
        return at, q, do, p.astype(BF16), (p * dp).astype(BF16)

    dk, dv = None, None
    pieces = rows // SUB
    later = front(0)
    terms = []
    for i in range(pieces):
        at, q, do, p, ds = later
        if i + 1 < pieces:
            later = front(i + 1)
        yield_dq = dot(ds, key, 1, 0)
        terms.append((at, yield_dq))
        part_v, part_k = dot(do, p, 0, 0), dot(q, ds, 0, 0)
        dv = part_v if dv is None else dv + part_v
        dk = part_k if dk is None else dk + part_k
    return terms, dk, dv


def far_kernel(row, has_dq, has_g, has_low, code_ref, rows_ref, kv_ref, *refs):
    refs = list(refs)
    dq_in = refs.pop(0) if has_dq else None
    g_in = refs.pop(0) if has_g else None
    low_ref = refs.pop() if has_low else None
    dq_ref, g_ref = refs[-2:]
    depth = kv_ref.shape[1]
    tokens = kv_ref.shape[0] // 2
    span = tokens // 2
    half = rows_ref.shape[0] // 6
    code = read_code(code_ref, row)
    every = code == 15

    def put(rows, lanes, value):
        if has_g:
            value = value + g_in[rows, lanes]
        g_ref[rows, lanes] = value.astype(g_ref.dtype)

    def run(base, count, at, keys, lanes, store=False):
        key, value = kv_ref[pl.ds(at, keys), :], kv_ref[pl.ds(at + tokens, keys), :]
        terms, dk, dv = tile(rows_ref, key, value, base, count)
        for rows_at, term in terms:
            dq_ref[rows_at, :] = term if store else dq_ref[rows_at, :] + term
        put(pl.ds(0, depth), lanes, dk)
        put(pl.ds(depth, depth), lanes, dv)

    @pl.when(every)
    def _():
        run(0, 2 * half, 0, tokens, pl.ds(0, tokens), store=not has_dq)

    def one_span(j, carry):
        bits = jnp.where(j == 0, code, code // 4)
        at = pl.multiple_of(j * span, span)
        lanes = pl.ds(at, span)
        a0, a1 = bits % 2 == 1, (bits // 2) % 2 == 1

        @pl.when(a0 & a1)
        def _():
            run(0, 2 * half, at, span, lanes)

        @pl.when(a0 != a1)
        def _():
            run(jnp.where(a1, half, 0), half, at, span, lanes)

        @pl.when(~(a0 | a1))
        def _():
            put(pl.ds(0, 2 * depth), lanes, jnp.zeros((2 * depth, span), F32))

        return carry

    @pl.when(~every)
    def _():
        if not has_dq:
            dq_ref[...] = jnp.zeros_like(dq_ref)
        lax.fori_loop(0, 2, one_span, 0)

    if has_low:
        low_ref[...] = dq_ref[...].astype(BF16)


def far(row, codes, q_rows, kv, name, dq=None, g=None, dtype=F32, low=False, weight=10):
    rows, depth = q_rows.shape[0] // 3, q_rows.shape[1]
    tokens = kv.shape[0] // 2
    args = [codes, q_rows, kv] + [a for a in (dq, g) if a is not None]
    wide = jax.ShapeDtypeStruct((rows, depth), F32)
    return pl.pallas_call(
        functools.partial(far_kernel, row, dq is not None, g is not None, low),
        out_shape=[wide, jax.ShapeDtypeStruct((2 * depth, tokens), dtype)]
        + ([jax.ShapeDtypeStruct((rows, depth), BF16)] if low else []),
        in_specs=[VMEM] * len(args),
        out_specs=[VMEM] * (3 if low else 2),
        input_output_aliases={} if dq is None else {3: 0},
        compiler_params=pltpu.CompilerParams(vmem_limit_bytes=24 * 2**20),
        cost_estimate=pl.CostEstimate(
            flops=weight * rows * tokens * depth,
            bytes_accessed=2**16,
            transcendentals=weight * rows * tokens // 10,
        ),
        name=name,
    )(*args)


def own_low_kernel(code_ref, rows_ref, kv_ref, _, __, dq_ref, g_ref):
    depth = kv_ref.shape[1]
    tokens = kv_ref.shape[0] // 2
    span, half = tokens // 2, rows_ref.shape[0] // 6
    heads = half // span
    low = read_code(code_ref, LOW)

    def causal(base, rows, keys):
        row = lax.broadcasted_iota(jnp.int32, (rows, keys), 0)
        return heads * lax.broadcasted_iota(jnp.int32, (rows, keys), 1) - row <= base

    at = pl.multiple_of(low * span, span)
    key, value = kv_ref[pl.ds(at, span), :], kv_ref[pl.ds(at + tokens, span), :]
    terms, dk, dv = tile(rows_ref, key, value, low * half, half, causal)
    for rows_at, term in terms:
        dq_ref[rows_at, :] += term
    g_ref[0:depth, :] = dk
    g_ref[depth : 2 * depth, :] = dv


def own_high_kernel(code_ref, rows_ref, kv_ref, g_low_ref, _, dq_ref, g_ref):
    depth = kv_ref.shape[1]
    tokens = kv_ref.shape[0] // 2
    span, half = tokens // 2, rows_ref.shape[0] // 6
    heads = half // span
    low = read_code(code_ref, LOW)

    def causal(base, rows, keys):
        row = lax.broadcasted_iota(jnp.int32, (rows, keys), 0)
        slot = lax.broadcasted_iota(jnp.int32, (1, keys), 1)
        own = (slot >= span) == (low == 0)
        return jnp.where(own, heads * (slot & (span - 1)), -1) - row <= base

    terms, dk, dv = tile(
        rows_ref, kv_ref[0:tokens, :], kv_ref[tokens : 2 * tokens, :],
        (1 - low) * half, half, causal,
    )
    for rows_at, term in terms:
        dq_ref[rows_at, :] += term
    g_ref[0:depth, :] = dk
    g_ref[depth : 2 * depth, :] = dv
    lanes = pl.ds(pl.multiple_of(low * span, span), span)
    g_ref[:, lanes] += g_low_ref[...]


def own(kernel, codes, q_rows, kv, extra, dq, keys, name, weight):
    rows, depth = dq.shape
    args = [codes, q_rows, kv] + extra + [dq]
    return pl.pallas_call(
        kernel,
        out_shape=[
            jax.ShapeDtypeStruct((rows, depth), F32),
            jax.ShapeDtypeStruct((2 * depth, keys), F32),
        ],
        in_specs=[VMEM] * len(args),
        out_specs=[VMEM, VMEM],
        input_output_aliases={len(args) - 1: 0},
        compiler_params=pltpu.CompilerParams(vmem_limit_bytes=24 * 2**20),
        cost_estimate=pl.CostEstimate(
            flops=weight * rows * keys * depth // 10, bytes_accessed=2**16, transcendentals=rows * keys // 100
        ),
        name=name,
    )(*args)


def finish_kernel(dq_ref, mate_ref, o_ref):
    total = dq_ref[...] + mate_ref[...].astype(F32)
    o_ref[...] = (total * float(dq_ref.shape[1] ** -0.5)).astype(BF16)


def finish(dq, mate):
    return pl.pallas_call(
        finish_kernel,
        out_shape=jax.ShapeDtypeStruct(dq.shape, BF16),
        in_specs=[VMEM, VMEM],
        out_specs=VMEM,
        compiler_params=pltpu.CompilerParams(vmem_limit_bytes=8 * 2**20),
        cost_estimate=pl.CostEstimate(flops=dq.size, bytes_accessed=6 * dq.size, transcendentals=0),
        name="finish",
    )(dq, mate)


def merge_kernel(own_ref, a_ref, b_ref, c_ref, _, keep_ref, send_ref):
    rows, tokens = own_ref.shape
    half = tokens // 2
    head = lax.axis_index("head")

    def part(index):
        lanes = pl.ds(pl.multiple_of(index * half, half), half)
        return (
            own_ref[:, lanes]
            + a_ref[:, lanes].astype(F32)
            + b_ref[:, lanes].astype(F32)
            + c_ref[:, lanes]
        )

    send_ref[...] = part(1 - head).astype(BF16)
    keep_ref[...] = part(head)


def merge(g, a, b, c, after):
    rows, tokens = g.shape
    return pl.pallas_call(
        merge_kernel,
        out_shape=[
            jax.ShapeDtypeStruct((rows, tokens // 2), F32),
            jax.ShapeDtypeStruct((rows, tokens // 2), BF16),
        ],
        in_specs=[VMEM] * 4 + [pl.BlockSpec(memory_space=pltpu.HBM)],
        out_specs=[VMEM, VMEM],
        compiler_params=pltpu.CompilerParams(vmem_limit_bytes=8 * 2**20),
        name="merge",
    )(g, a, b, c, pltpu.with_memory_space_constraint(after, pltpu.HBM))


def last_kernel(keep_ref, got_ref, dk_ref, dv_ref):
    total = keep_ref[...] + got_ref[1 - lax.axis_index("head")].astype(F32)
    depth = total.shape[0] // 2
    dk_ref[...] = (total[:depth].T * float(depth**-0.5)).astype(BF16)
    dv_ref[...] = total[depth:].T.astype(BF16)


def last(keep, got):
    rows, tokens = keep.shape
    shape = jax.ShapeDtypeStruct((tokens, rows // 2), BF16)
    return pl.pallas_call(
        last_kernel,
        out_shape=[shape, shape],
        in_specs=[VMEM, VMEM],
        out_specs=[VMEM, VMEM],
        compiler_params=pltpu.CompilerParams(vmem_limit_bytes=8 * 2**20),
        name="last",
    )(keep, got)


def ring(count, move):
    pairs = []
    for d in range(count):
        target = move(d)
        flip = 0 if 0 <= target < count else 1
        for h in range(2):
            pairs.append((2 * d + h, 2 * (target % count) + (h ^ flip)))
    return pairs


def local(queries, keys, values, outputs, grad_out, lse, span_order):
    tokens, heads, depth = queries.shape
    count = lax.axis_size("ctx")
    both = ("ctx", "head")
    q = queries.reshape(tokens * heads, depth)
    do = grad_out.reshape(tokens * heads, depth)
    out = outputs.reshape(tokens * heads, depth)
    over_two = ring(count, lambda d: d - 2 if d % 2 else d + 2)
    back_two = [(b, a) for a, b in over_two]
    over_one = ring(count, lambda d: d + 1 if d % 2 else d - 1)
    mates = [(d, d ^ 1) for d in range(count)]

    kv, q_rows, out, codes = load(span_order, keys, values, q, do, out)
    kv_a = lax.ppermute(kv, both, over_two)
    kv_b = lax.ppermute(kv, both, over_one)
    q_rows = prep(q_rows, out, lse)
    mate_rows = lax.ppermute(q_rows, "ctx", mates)

    dq, g_a = far(0, codes, q_rows, kv_a, "far_a", dtype=BF16)
    got_a = lax.ppermute(g_a, both, back_two)
    dq, g_b = far(1, codes, q_rows, kv_b, "far_b", dq=dq, weight=1000)
    dq_mate, g_mate = far(3, codes, mate_rows, kv, "own_mate")
    _, g_b, dq_low = far(
        2, codes, mate_rows, kv_b, "far_b_mate", dq=dq_mate, g=g_b, dtype=BF16, low=True
    )
    got_b = lax.ppermute(g_b, both, over_one)
    got_dq = lax.ppermute(dq_low, "ctx", mates)
    dq, g_low = own(own_low_kernel, codes, q_rows, kv, [got_a], dq, tokens // 2, "own_low", 600)
    dq, g_own = own(own_high_kernel, codes, q_rows, kv, [g_low], dq, tokens, "own_high", 1)
    grad_q = finish(dq, got_dq)
    keep, send = merge(g_own, got_a, got_b, g_mate, grad_q)
    got = lax.all_gather(send, "head")
    grad_k, grad_v = last(keep, got)
    return grad_q.reshape(tokens, heads, depth), grad_k, grad_v


def solution(mesh):
    return jax.shard_map(
        local,
        mesh=mesh,
        in_specs=(
            P("ctx", "head", None),
            P("ctx", None),
            P("ctx", None),
            P("ctx", "head", None),
            P("ctx", "head", None),
            P("head", "ctx"),
            P(),
        ),
        out_specs=(P("ctx", "head", None), P(("ctx", "head"), None), P(("ctx", "head"), None)),
        check_vma=False,
    )
```

```python
import functools

import jax
import jax.numpy as jnp
from jax import lax
from jax.experimental import pallas as pl
from jax.experimental.pallas import tpu as pltpu
from jax.sharding import PartitionSpec as P

F32 = jnp.float32
BF16 = jnp.bfloat16
LOG2E = 1.4426950408889634
SUB = 512
LOW = 4
VMEM = pl.BlockSpec(memory_space=pltpu.VMEM)
SMEM = pl.BlockSpec(memory_space=pltpu.SMEM)


def dot(a, b, ca, cb):
    return lax.dot_general(a, b, (((ca,), (cb,)), ((), ())), preferred_element_type=F32)


def lane_ones(rows, low, high):
    lane = lax.broadcasted_iota(jnp.int32, (rows, 128), 1)
    return jnp.where((lane >= low) & (lane < high), 1.0, 0.0).astype(BF16)


def load_kernel(
    span_from, k_ref, v_ref, q_ref, do_ref, out_ref, kv_to, rows_to, out_to, code_ref, span_ref, sems
):
    tokens, rows = k_ref.shape[0], q_ref.shape[0]
    copies = [
        pltpu.make_async_copy(source, target, sems.at[i])
        for i, (source, target) in enumerate(
            [
                (span_from, span_ref),
                (k_ref, kv_to.at[pl.ds(0, tokens)]),
                (v_ref, kv_to.at[pl.ds(tokens, tokens)]),
                (do_ref, rows_to.at[pl.ds(rows, rows)]),
                (out_ref, out_to),
                (q_ref, rows_to.at[pl.ds(0, rows)]),
            ]
        )
    ]
    for copy in copies:
        copy.start()
    copies[0].wait()
    count = lax.axis_size("ctx")
    me = lax.axis_index("ctx")
    sign = 1 - 2 * (me % 2)
    mate, near, far = me + sign, (me - sign + count) % count, (me - 2 * sign + count) % count
    row = lax.broadcasted_iota(jnp.int32, code_ref.shape, 0)
    later = span_ref[2 * me] > span_ref[2 * me + 1]
    codes = jnp.where(row == LOW, jnp.where(later, 1.0, 0.0), 0.0)
    for r, (query, source) in enumerate(((me, far), (me, near), (mate, near), (mate, me))):
        q0, q1 = span_ref[2 * query], span_ref[2 * query + 1]
        k0, k1 = span_ref[2 * source], span_ref[2 * source + 1]
        code = 0.0
        for bit, allowed in enumerate((k0 < q0, k0 < q1, k1 < q0, k1 < q1)):
            code = code + jnp.where(allowed, float(2**bit), 0.0)
        codes = jnp.where(row == r, code, codes)
    code_ref[...] = codes
    for copy in copies[1:]:
        copy.wait()


def load(spans, keys, values, q, do, out):
    tokens, depth = keys.shape
    rows = q.shape[0]
    args = [pltpu.with_memory_space_constraint(a, pltpu.HBM) for a in (spans, keys, values, q, do, out)]
    return pl.pallas_call(
        load_kernel,
        out_shape=[
            jax.ShapeDtypeStruct((2 * tokens, depth), BF16),
            jax.ShapeDtypeStruct((3 * rows, depth), BF16),
            jax.ShapeDtypeStruct((rows, depth), BF16),
            jax.ShapeDtypeStruct((8, 128), F32),
        ],
        in_specs=[pl.BlockSpec(memory_space=pltpu.HBM)] * 6,
        out_specs=[VMEM] * 4,
        scratch_shapes=[pltpu.SMEM(spans.shape, jnp.int32), pltpu.SemaphoreType.DMA((6,))],
        compiler_params=pltpu.CompilerParams(vmem_limit_bytes=8 * 2**20),
        name="load",
    )(*args)


def prep_kernel(rows_in_ref, out_ref, lse_ref, rows_ref, wide):
    rows = out_ref.shape[0]
    heads, tokens = lse_ref.shape
    depth = out_ref.shape[1]
    lse = lse_ref[...] * float(depth**0.5)
    turned = jnp.concatenate([lse, jnp.zeros((128 - heads, tokens), F32)], axis=0).T
    for g in range(heads):
        wide[pl.ds(g, tokens, stride=heads), :] = jnp.broadcast_to(
            turned[:, g : g + 1], (tokens, 128)
        )
    delta = jnp.sum(
        rows_in_ref[rows : 2 * rows, :].astype(F32) * out_ref[...].astype(F32), axis=1, keepdims=True
    )
    lane = lax.broadcasted_iota(jnp.int32, wide.shape, 1)
    rest = jnp.where(lane < 3, wide[...], delta)
    high = rest.astype(BF16).astype(F32)
    rest = rest - high
    mid = rest.astype(BF16).astype(F32)
    low = rest - mid
    place = jnp.where(lane < 3, lane, lane - 3)
    term = jnp.where(place == 0, high, jnp.where(place == 1, mid, low))
    rows_ref[2 * rows : 3 * rows, :] = jnp.where(lane < 6, -term, 0.0).astype(BF16)


def read_code(code_ref, row):
    return jnp.max(code_ref[pl.ds(row, 1), :]).astype(jnp.int32)


def prep(q_rows, out_rows, lse):
    rows = out_rows.shape[0]
    return pl.pallas_call(
        prep_kernel,
        out_shape=jax.ShapeDtypeStruct(q_rows.shape, BF16),
        in_specs=[VMEM] * 3,
        out_specs=VMEM,
        input_output_aliases={0: 0},
        scratch_shapes=[pltpu.VMEM((rows, 128), F32)],
        compiler_params=pltpu.CompilerParams(vmem_limit_bytes=16 * 2**20),
        cost_estimate=pl.CostEstimate(flops=rows * 1024, bytes_accessed=rows * 768, transcendentals=0),
        name="prep",
    )(q_rows, out_rows, lse)


def tile(rows_ref, key, value, q_base, rows, mask=None):
    span, depth = key.shape
    count = rows_ref.shape[0] // 3
    exponent = float(depth**-0.5 * LOG2E)
    key_x = jnp.concatenate([key, lane_ones(span, 0, 3)], axis=1)
    value_x = jnp.concatenate([value, lane_ones(span, 3, 6)], axis=1)

    def front(i):
        first = pl.multiple_of(q_base + i * SUB, SUB)
        at = pl.ds(first, SUB)
        q, do, x = (rows_ref[pl.ds(first + part * count, SUB), :] for part in range(3))
        p = jnp.exp2(dot(jnp.concatenate([q, x], axis=1), key_x, 1, 1) * exponent)
        if mask is not None:
            p = jnp.where(mask(i * SUB, SUB, span), p, 0.0)
        dp = dot(jnp.concatenate([do, x], axis=1), value_x, 1, 1)
        return at, q, do, p.astype(BF16), (p * dp).astype(BF16)

    dk, dv = None, None
    pieces = rows // SUB
    later = front(0)
    terms = []
    for i in range(pieces):
        at, q, do, p, ds = later
        if i + 1 < pieces:
            later = front(i + 1)
        yield_dq = dot(ds, key, 1, 0)
        terms.append((at, yield_dq))
        part_v, part_k = dot(do, p, 0, 0), dot(q, ds, 0, 0)
        dv = part_v if dv is None else dv + part_v
        dk = part_k if dk is None else dk + part_k
    return terms, dk, dv


def far_kernel(row, has_dq, has_g, has_low, code_ref, rows_ref, kv_ref, *refs):
    refs = list(refs)
    dq_in = refs.pop(0) if has_dq else None
    g_in = refs.pop(0) if has_g else None
    low_ref = refs.pop() if has_low else None
    dq_ref, g_ref = refs[-2:]
    depth = kv_ref.shape[1]
    tokens = kv_ref.shape[0] // 2
    span = tokens // 2
    half = rows_ref.shape[0] // 6
    code = read_code(code_ref, row)
    every = code == 15

    def put(rows, lanes, value):
        if has_g:
            value = value + g_in[rows, lanes]
        g_ref[rows, lanes] = value.astype(g_ref.dtype)

    def run(base, count, at, keys, lanes, store=False):
        key, value = kv_ref[pl.ds(at, keys), :], kv_ref[pl.ds(at + tokens, keys), :]
        terms, dk, dv = tile(rows_ref, key, value, base, count)
        for rows_at, term in terms:
            dq_ref[rows_at, :] = term if store else dq_ref[rows_at, :] + term
        put(pl.ds(0, depth), lanes, dk)
        put(pl.ds(depth, depth), lanes, dv)

    @pl.when(every)
    def _():
        run(0, 2 * half, 0, tokens, pl.ds(0, tokens), store=not has_dq)

    def one_span(j, carry):
        bits = jnp.where(j == 0, code, code // 4)
        at = pl.multiple_of(j * span, span)
        lanes = pl.ds(at, span)
        a0, a1 = bits % 2 == 1, (bits // 2) % 2 == 1

        @pl.when(a0 & a1)
        def _():
            run(0, 2 * half, at, span, lanes)

        @pl.when(a0 != a1)
        def _():
            run(jnp.where(a1, half, 0), half, at, span, lanes)

        @pl.when(~(a0 | a1))
        def _():
            put(pl.ds(0, 2 * depth), lanes, jnp.zeros((2 * depth, span), F32))

        return carry

    @pl.when(~every)
    def _():
        if not has_dq:
            dq_ref[...] = jnp.zeros_like(dq_ref)
        lax.fori_loop(0, 2, one_span, 0)

    if has_low:
        low_ref[...] = dq_ref[...].astype(BF16)


def far(row, codes, q_rows, kv, name, dq=None, g=None, dtype=F32, low=False, weight=10):
    rows, depth = q_rows.shape[0] // 3, q_rows.shape[1]
    tokens = kv.shape[0] // 2
    args = [codes, q_rows, kv] + [a for a in (dq, g) if a is not None]
    wide = jax.ShapeDtypeStruct((rows, depth), F32)
    return pl.pallas_call(
        functools.partial(far_kernel, row, dq is not None, g is not None, low),
        out_shape=[wide, jax.ShapeDtypeStruct((2 * depth, tokens), dtype)]
        + ([jax.ShapeDtypeStruct((rows, depth), BF16)] if low else []),
        in_specs=[VMEM] * len(args),
        out_specs=[VMEM] * (3 if low else 2),
        input_output_aliases={} if dq is None else {3: 0},
        compiler_params=pltpu.CompilerParams(vmem_limit_bytes=24 * 2**20),
        cost_estimate=pl.CostEstimate(
            flops=weight * rows * tokens * depth,
            bytes_accessed=2**16,
            transcendentals=weight * rows * tokens // 10,
        ),
        name=name,
    )(*args)


def own_low_kernel(code_ref, rows_ref, kv_ref, _, __, dq_ref, g_ref):
    depth = kv_ref.shape[1]
    tokens = kv_ref.shape[0] // 2
    span, half = tokens // 2, rows_ref.shape[0] // 6
    heads = half // span
    low = read_code(code_ref, LOW)

    def causal(base, rows, keys):
        row = lax.broadcasted_iota(jnp.int32, (rows, keys), 0)
        return heads * lax.broadcasted_iota(jnp.int32, (rows, keys), 1) - row <= base

    at = pl.multiple_of(low * span, span)
    key, value = kv_ref[pl.ds(at, span), :], kv_ref[pl.ds(at + tokens, span), :]
    terms, dk, dv = tile(rows_ref, key, value, low * half, half, causal)
    for rows_at, term in terms:
        dq_ref[rows_at, :] += term
    g_ref[0:depth, :] = dk
    g_ref[depth : 2 * depth, :] = dv


def own_high_kernel(code_ref, rows_ref, kv_ref, g_low_ref, _, dq_ref, g_ref):
    depth = kv_ref.shape[1]
    tokens = kv_ref.shape[0] // 2
    span, half = tokens // 2, rows_ref.shape[0] // 6
    heads = half // span
    low = read_code(code_ref, LOW)

    def causal(base, rows, keys):
        row = lax.broadcasted_iota(jnp.int32, (rows, keys), 0)
        slot = lax.broadcasted_iota(jnp.int32, (1, keys), 1)
        own = (slot >= span) == (low == 0)
        return jnp.where(own, heads * (slot & (span - 1)), -1) - row <= base

    terms, dk, dv = tile(
        rows_ref, kv_ref[0:tokens, :], kv_ref[tokens : 2 * tokens, :],
        (1 - low) * half, half, causal,
    )
    for rows_at, term in terms:
        dq_ref[rows_at, :] += term
    g_ref[0:depth, :] = dk
    g_ref[depth : 2 * depth, :] = dv
    lanes = pl.ds(pl.multiple_of(low * span, span), span)
    g_ref[:, lanes] += g_low_ref[...]


def own(kernel, codes, q_rows, kv, extra, dq, keys, name, weight):
    rows, depth = dq.shape
    args = [codes, q_rows, kv] + extra + [dq]
    return pl.pallas_call(
        kernel,
        out_shape=[
            jax.ShapeDtypeStruct((rows, depth), F32),
            jax.ShapeDtypeStruct((2 * depth, keys), F32),
        ],
        in_specs=[VMEM] * len(args),
        out_specs=[VMEM, VMEM],
        input_output_aliases={len(args) - 1: 0},
        compiler_params=pltpu.CompilerParams(vmem_limit_bytes=24 * 2**20),
        cost_estimate=pl.CostEstimate(
            flops=weight * rows * keys * depth // 10, bytes_accessed=2**16, transcendentals=rows * keys // 100
        ),
        name=name,
    )(*args)


def finish_kernel(dq_ref, mate_ref, o_ref):
    total = dq_ref[...] + mate_ref[...].astype(F32)
    o_ref[...] = (total * float(dq_ref.shape[1] ** -0.5)).astype(BF16)


def finish(dq, mate):
    return pl.pallas_call(
        finish_kernel,
        out_shape=jax.ShapeDtypeStruct(dq.shape, BF16),
        in_specs=[VMEM, VMEM],
        out_specs=VMEM,
        compiler_params=pltpu.CompilerParams(vmem_limit_bytes=8 * 2**20),
        cost_estimate=pl.CostEstimate(flops=dq.size, bytes_accessed=6 * dq.size, transcendentals=0),
        name="finish",
    )(dq, mate)


def merge_kernel(own_ref, a_ref, b_ref, c_ref, _, keep_ref, send_ref):
    rows, tokens = own_ref.shape
    half = tokens // 2
    head = lax.axis_index("head")

    def part(index):
        lanes = pl.ds(pl.multiple_of(index * half, half), half)
        return (
            own_ref[:, lanes]
            + a_ref[:, lanes].astype(F32)
            + b_ref[:, lanes].astype(F32)
            + c_ref[:, lanes]
        )

    send_ref[...] = part(1 - head).astype(BF16)
    keep_ref[...] = part(head)


def merge(g, a, b, c, after):
    rows, tokens = g.shape
    return pl.pallas_call(
        merge_kernel,
        out_shape=[
            jax.ShapeDtypeStruct((rows, tokens // 2), F32),
            jax.ShapeDtypeStruct((rows, tokens // 2), BF16),
        ],
        in_specs=[VMEM] * 4 + [pl.BlockSpec(memory_space=pltpu.HBM)],
        out_specs=[VMEM, VMEM],
        compiler_params=pltpu.CompilerParams(vmem_limit_bytes=8 * 2**20),
        name="merge",
    )(g, a, b, c, pltpu.with_memory_space_constraint(after, pltpu.HBM))


def last_kernel(keep_ref, got_ref, dk_ref, dv_ref):
    total = keep_ref[...] + got_ref[1 - lax.axis_index("head")].astype(F32)
    depth = total.shape[0] // 2
    dk_ref[...] = (total[:depth].T * float(depth**-0.5)).astype(BF16)
    dv_ref[...] = total[depth:].T.astype(BF16)


def last(keep, got):
    rows, tokens = keep.shape
    shape = jax.ShapeDtypeStruct((tokens, rows // 2), BF16)
    return pl.pallas_call(
        last_kernel,
        out_shape=[shape, shape],
        in_specs=[VMEM, VMEM],
        out_specs=[VMEM, VMEM],
        compiler_params=pltpu.CompilerParams(vmem_limit_bytes=8 * 2**20),
        name="last",
    )(keep, got)


def ring(count, move):
    pairs = []
    for d in range(count):
        target = move(d)
        flip = 0 if 0 <= target < count else 1
        for h in range(2):
            pairs.append((2 * d + h, 2 * (target % count) + (h ^ flip)))
    return pairs


def local(queries, keys, values, outputs, grad_out, lse, span_order):
    tokens, heads, depth = queries.shape
    count = lax.axis_size("ctx")
    both = ("ctx", "head")
    q = queries.reshape(tokens * heads, depth)
    do = grad_out.reshape(tokens * heads, depth)
    out = outputs.reshape(tokens * heads, depth)
    over_two = ring(count, lambda d: d - 2 if d % 2 else d + 2)
    back_two = [(b, a) for a, b in over_two]
    over_one = ring(count, lambda d: d + 1 if d % 2 else d - 1)
    mates = [(d, d ^ 1) for d in range(count)]

    kv, q_rows, out, codes = load(span_order, keys, values, q, do, out)
    kv_a = lax.ppermute(kv, "ctx", [(d, (d - 2 if d % 2 else d + 2) % count) for d in range(count)])
    kv_b = lax.ppermute(kv, "ctx", [(d, (d + 1 if d % 2 else d - 1) % count) for d in range(count)])
    q_rows = prep(q_rows, out, lse)
    mate_rows = lax.ppermute(q_rows, "ctx", mates)

    dq, g_a = far(0, codes, q_rows, kv_a, "far_a", dtype=BF16)
    got_a = lax.ppermute(g_a, both, back_two)
    dq, g_b = far(1, codes, q_rows, kv_b, "far_b", dq=dq, weight=1000)
    dq_mate, g_mate = far(3, codes, mate_rows, kv, "own_mate")
    _, g_b, dq_low = far(
        2, codes, mate_rows, kv_b, "far_b_mate", dq=dq_mate, g=g_b, dtype=BF16, low=True
    )
    got_b = lax.ppermute(g_b, both, over_one)
    got_dq = lax.ppermute(dq_low, "ctx", mates)
    dq, g_low = own(own_low_kernel, codes, q_rows, kv, [got_a], dq, tokens // 2, "own_low", 600)
    dq, g_own = own(own_high_kernel, codes, q_rows, kv, [g_low], dq, tokens, "own_high", 1)
    grad_q = finish(dq, got_dq)
    keep, send = merge(g_own, got_a, got_b, g_mate, grad_q)
    got = lax.all_gather(send, "head")
    grad_k, grad_v = last(keep, got)
    return grad_q.reshape(tokens, heads, depth), grad_k, grad_v


def solution(mesh):
    return jax.shard_map(
        local,
        mesh=mesh,
        in_specs=(
            P("ctx", "head", None),
            P("ctx", None),
            P("ctx", None),
            P("ctx", "head", None),
            P("ctx", "head", None),
            P("head", "ctx"),
            P(),
        ),
        out_specs=(P("ctx", "head", None), P(("ctx", "head"), None), P(("ctx", "head"), None)),
        check_vma=False,
    )
```
